128 devices in a mesh: dp: 32 (over z, y, core), tensor: 4 (over x).
Axes of the slice: x: 4, y: 4, z: 4, core: 2. Of those that a mesh axis runs over, the one named last changes fastest.
Arguments:
- tokens: bfloat16 [16384, 768], P(('dp', 'tensor')), may hold values from -6 to 6
- lengths: int32 [32, 3], P('dp'), may hold values from 1 to 384, 512 in all within a row
- norm_gain: float32 [2, 768], replicated, may hold values from 0.5 to 1.5
- w_zx: bfloat16 [2, 768, 2, 1536], P(None, 'dp', None, 'tensor'), may hold values from -0.21875 to 0.21875
- w_bc: bfloat16 [2, 768, 256], P(None, 'dp'), may hold values from -0.21875 to 0.21875
- w_dt: bfloat16 [2, 768, 24], P(None, 'dp', 'tensor'), may hold values from -0.21875 to 0.21875
- conv_x: bfloat16 [2, 5, 24, 64], P(None, None, 'tensor', 'dp'), may hold values from -3 to 3
- conv_bc: bfloat16 [2, 5, 256], P(None, None, 'dp'), may hold values from -3 to 3
- a_log: float32 [2, 24], P(None, 'tensor'), may hold values from 0 to 1.5
- dt_bias: float32 [2, 24], P(None, 'tensor'), may hold values from -7 to -2
- d_skip: float32 [2, 24], P(None, 'tensor'), may hold values from 0.5 to 1.5
- gate_gain: bfloat16 [2, 24, 64], P(None, 'tensor', 'dp'), may hold values from 0.5 to 1.5
- w_out: bfloat16 [2, 1536, 768], P(None, 'tensor', 'dp'), may hold values from -0.15625 to 0.15625
- cotangent: bfloat16 [16384, 768], P(('dp', 'tensor')), may hold values from -6 to 6
Outputs:
- block_out: bfloat16 [16384, 768], P(('dp', 'tensor'))
- input_grad: float32 [16384, 768], P(('dp', 'tensor'))
- grad_norm_gain: float32 [2, 768], replicated
- grad_w_zx: float32 [2, 768, 2, 1536], P(None, 'dp', None, 'tensor')
- grad_w_bc: float32 [2, 768, 256], P(None, 'dp')
- grad_w_dt: float32 [2, 768, 24], P(None, 'dp', 'tensor')
- grad_conv_x: float32 [2, 5, 24, 64], P(None, None, 'tensor', 'dp')
- grad_conv_bc: float32 [2, 5, 256], P(None, None, 'dp')
- grad_a_log: float32 [2, 24], P(None, 'tensor')
- grad_dt_bias: float32 [2, 24], P(None, 'tensor')
- grad_d_skip: float32 [2, 24], P(None, 'tensor')
- grad_gate_gain: float32 [2, 24, 64], P(None, 'tensor', 'dp')
- grad_w_out: float32 [2, 1536, 768], P(None, 'tensor', 'dp')
The draws below stay inside these ranges and needn't reach their ends.
Inputs may be any that keep to these rules, and one draw needn't show every extreme that they name: `lengths`: each row sums to 512, and its largest entry is exactly 384.
All inputs are finite; a program needn't handle non-finite values.
Results may differ from the reference program's by a relative error of at most 0.035.
Values may be sent and summed in bfloat16 or wider, within the bound.
A program may use at most 128 MiB of HBM per device.

```python
import math
import jax
import jax.numpy as jnp
import numpy as np
from jax import lax

D = 768
HEADS = 24
P_SIZE = 64
N = 128
K = 4
STRETCH = 256
LAYERS = 2
SEQS = 3
DI = 1536
GROUP_TOK = 512
MOST_LEN = 384
TOKENS = 16384
N_DP = 32


def block_levels(own_key, extent, cuts, low, largest):
    factor_of = 1.0
    for dim, shards_of in cuts:
        draws = jax.random.uniform(jax.random.fold_in(jax.random.fold_in(own_key, 6), dim), (shards_of,), jnp.float32, low / len(cuts), largest / len(cuts))
        factor_of = factor_of * jnp.repeat(jnp.exp(draws), extent[dim] // shards_of).reshape((-1,) + (1,) * (len(extent) - 1 - dim))
    return factor_of


def split_up(count, total, limit, lean):
    loads = [(1 << 20) // math.isqrt(rank ** lean) + 1 for rank in range(2, count + 1)]
    surplus, holding = total - limit - (count - 1), [1] * (count - 1)
    while surplus > 0:
        free = [i for i in range(count - 1) if holding[i] < limit]
        mass, left = sum([loads[i] for i in free]), surplus
        for i in free:
            more = min(limit - holding[i], max(1, left * loads[i] // mass), surplus)
            holding[i] = holding[i] + more
            surplus = surplus - more
    return np.array([limit] + holding)


def uneven(rng, amount, total, limit, skew):
    if amount == 2:
        one = jax.random.randint(rng, (), max(1, total - limit), min(limit, total - 1) + 1)
        return jnp.stack([one, total - one])
    sizes = jnp.asarray(split_up(amount, total, limit, skew), jnp.int32)
    pairs = (amount - 1) // 2
    giver, receiver = sizes[1:1 + 2 * pairs:2], sizes[2:2 + 2 * pairs:2]
    margin = jnp.minimum(giver - 1, limit - receiver)
    moved = jax.random.randint(jax.random.fold_in(rng, 1), (pairs,), 0, 1 << 20) % (margin + 1)
    sizes = sizes.at[1:1 + 2 * pairs:2].set(giver - moved).at[2:2 + 2 * pairs:2].set(receiver + moved)
    return sizes[jax.random.permutation(jax.random.fold_in(rng, 2), amount)]


def scatter_about(rng, shape, deviation, reach, split=(), kind=jnp.bfloat16):
    level = block_levels(rng, shape, split, -0.22, 0.18) if split else 1.0
    values = jax.random.normal(rng, shape, jnp.float32) * deviation * level
    return jnp.minimum(jnp.maximum(values, -reach), reach).astype(kind)


def setup_inputs(seed: int = 0) -> dict:
    key_of = jax.random.split(jax.random.key(seed), 15)
    tokens = scatter_about(key_of[0], (TOKENS, D), 1.0, 6.0, ((0, 128),))
    lengths = jax.vmap(lambda own: uneven(own, SEQS, GROUP_TOK, MOST_LEN, 2))(jax.random.split(key_of[1], N_DP)).reshape((N_DP, SEQS)).astype(jnp.int32)
    norm_gain = jnp.clip(1.0 + 0.1 * jax.random.normal(key_of[2], (LAYERS, D), jnp.float32), 0.5, 1.5)
    w_zx = scatter_about(key_of[3], (LAYERS, D, 2, DI), D ** -0.5, 0.21875, ((1, 32), (3, 4)))
    w_bc = scatter_about(key_of[4], (LAYERS, D, 2 * N), D ** -0.5, 0.21875, ((1, 32),))
    w_dt = scatter_about(key_of[5], (LAYERS, D, HEADS), D ** -0.5, 0.21875, ((1, 32), (2, 4)))
    conv_x = scatter_about(key_of[6], (LAYERS, K + 1, HEADS, P_SIZE), 0.5, 3.0, ((2, 4), (3, 32)))
    conv_bc = scatter_about(key_of[7], (LAYERS, K + 1, 2 * N), 0.5, 3.0, ((2, 32),))
    a_log = jnp.clip(1.5 * jax.random.uniform(key_of[8], (LAYERS, HEADS), jnp.float32) ** block_levels(key_of[8], (LAYERS, HEADS), ((1, 4),), -0.2, 0.2), 0.0, 1.5)
    dt_bias = jnp.clip(-7.0 + 5.0 * jax.random.uniform(key_of[9], (LAYERS, HEADS), jnp.float32) ** block_levels(key_of[9], (LAYERS, HEADS), ((1, 4),), -0.2, 0.2), -7.0, -2.0)
    d_skip = jnp.clip(0.5 + 1.0 * jax.random.uniform(key_of[10], (LAYERS, HEADS), jnp.float32) ** block_levels(key_of[10], (LAYERS, HEADS), ((1, 4),), -0.2, 0.2), 0.5, 1.5)
    gate_gain = jnp.clip(1.0 + 0.1 * jax.random.normal(key_of[11], (LAYERS, HEADS, P_SIZE), jnp.float32), 0.5, 1.5).astype(jnp.bfloat16)
    w_out = scatter_about(key_of[12], (LAYERS, DI, D), DI ** -0.5, 0.15625, ((1, 4), (2, 32)))
    cotangent = scatter_about(key_of[13], (TOKENS, D), 1.0, 6.0, ((0, 128),))
    return {"tokens": tokens, "lengths": lengths, "norm_gain": norm_gain, "w_zx": w_zx, "w_bc": w_bc, "w_dt": w_dt, "conv_x": conv_x, "conv_bc": conv_bc, "a_log": a_log, "dt_bias": dt_bias, "d_skip": d_skip, "gate_gain": gate_gain, "w_out": w_out, "cotangent": cotangent}


epsilon = 1e-05
highest = lax.Precision.HIGHEST

@jax.custom_vjp
def low(v):
    return lax.optimization_barrier(v.astype(jnp.bfloat16)).astype(jnp.float32)

@jax.custom_vjp
def low_back(v):
    return v

def low_keep(v):
    return (low(v), None)

def low_pass(kept, grad):
    return (grad,)

def back_keep(v):
    return (v, None)

def back_low(kept, grad):
    return (low(grad),)
low.defvjp(low_keep, low_pass)
low_back.defvjp(back_keep, back_low)

def rms_scale(values):
    return lax.rsqrt(lax.optimization_barrier(jnp.mean(values * values, axis=-1, keepdims=True)) + epsilon)

def segment_ids(pieces, length_all):
    endings = jnp.cumsum(pieces).astype(jnp.int32)
    places = jnp.arange(length_all, dtype=jnp.int32)
    return lax.optimization_barrier(jnp.sum((places[:, None] >= endings[None, :]).astype(jnp.int32), axis=1)).astype(jnp.int32)

def causal_conv(values, kernel, segments):
    length_all = values.shape[0]
    reach_back = kernel.shape[0] - 1
    padded = jnp.pad(values, ((reach_back - 1, 0), (0, 0)))
    padded_seg = jnp.pad(segments, (reach_back - 1, 0), constant_values=-1)
    summed = jnp.broadcast_to(kernel[reach_back][None, :], values.shape)
    for offset in range(reach_back):
        same_seg = (padded_seg[offset:offset + length_all] == segments)[:, None]
        summed = summed + jnp.where(same_seg, padded[offset:offset + length_all] * kernel[offset][None, :], 0.0)
    return summed

def scan_heads(signals, steps, rates, b_rows, c_rows, skips, segments):
    length_all, head_count, head_size = signals.shape
    blocks = length_all // STRETCH
    block_sig = signals.reshape(blocks, STRETCH, head_count, head_size)
    block_step = steps.reshape(blocks, STRETCH, head_count)
    block_b = b_rows.reshape(blocks, STRETCH, -1)
    block_c = c_rows.reshape(blocks, STRETCH, -1)
    block_seg = segments.reshape(blocks, STRETCH)
    logs_in = jnp.cumsum(block_step * rates[None, None, :], axis=1)
    places = jnp.arange(STRETCH)
    causal = places[:, None] >= places[None, :]
    linked_mask = ((block_seg[:, :, None] == block_seg[:, None, :]) & causal[None])[..., None]
    spread = logs_in[:, :, None, :] - logs_in[:, None, :, :]
    decays = jnp.where(linked_mask, jnp.exp(jnp.where(linked_mask, spread, 0.0)), 0.0)
    inner = jnp.einsum('bin,bjn->bij', block_c, block_b, precision=highest)
    mixing = inner[..., None] * decays * block_step[:, None, :, :]
    within = jnp.einsum('bijh,bjhp->bihp', mixing, block_sig, precision=highest)
    last_seg = block_seg[:, -1]
    last_log = logs_in[:, -1, :]
    tail_mask = (block_seg == last_seg[:, None])[..., None]
    to_end = jnp.where(tail_mask, jnp.exp(jnp.where(tail_mask, last_log[:, None, :] - logs_in, 0.0)), 0.0) * block_step
    weighted = to_end[..., None] * block_sig
    states = jnp.einsum('bjhp,bjn->bhpn', weighted, block_b, precision=highest)

    def carry_step(carried, inputs_now):
        carried_state, earlier_seg = carried
        block_state, block_last, block_log = inputs_now
        joined = (block_last == earlier_seg).astype(block_state.dtype)
        renewed = block_state + joined * jnp.exp(block_log)[:, None, None] * carried_state
        return ((renewed, block_last), (carried_state, earlier_seg))
    start_state = jnp.zeros(states.shape[1:], states.dtype)
    start_seg = jnp.array(-1, dtype=jnp.int32)
    unused_end, (incoming, earlier_segs) = lax.scan(carry_step, (start_state, start_seg), (states, last_seg, last_log))
    entering = (block_seg == earlier_segs[:, None])[..., None]
    reach_in = jnp.where(entering, jnp.exp(logs_in), 0.0)
    across = jnp.einsum('bin,bhpn->bihp', block_c, incoming, precision=highest) * reach_in[..., None]
    result = (within + across).reshape(length_all, head_count, head_size)
    return result + skips[None, :, None] * signals

def layer_group(stream, segments, gain, in_zx, in_bc, in_dt, kernel_x, kernel_bc, log_rates, step_bias, skip_gain, out_gain, out_weight):
    length_all = stream.shape[0]
    inner_units = HEADS * P_SIZE
    normed = low(stream * rms_scale(stream) * gain[None, :])
    both = low_back(jnp.dot(normed, in_zx.reshape(D, 2 * inner_units), precision=highest))
    gate_part = both[:, :inner_units]
    signal_part = both[:, inner_units:]
    b_and_c = low_back(jnp.dot(normed, in_bc, precision=highest))
    step_raw = low_back(jnp.dot(normed, in_dt, precision=highest))
    signals = low(jax.nn.silu(causal_conv(signal_part, kernel_x.reshape(K + 1, inner_units), segments)))
    b_and_c_act = low(jax.nn.silu(causal_conv(b_and_c, kernel_bc, segments)))
    steps = jax.nn.softplus(step_raw + step_bias[None, :])
    scanned = scan_heads(signals.reshape(length_all, HEADS, P_SIZE), steps, -jnp.exp(log_rates), b_and_c_act[:, :N], b_and_c_act[:, N:], skip_gain, segments)
    scanned = scanned.reshape(length_all, inner_units)
    gated = scanned * jax.nn.silu(gate_part)
    mixed = low(gated * rms_scale(gated) * out_gain.reshape(1, inner_units))
    branch = low_back(jnp.dot(mixed, out_weight, precision=highest))
    return stream + branch

def reference(tokens, lengths, norm_gain, w_zx, w_bc, w_dt, conv_x, conv_bc, a_log, dt_bias, d_skip, gate_gain, w_out, cotangent):
    groups = lengths.shape[0]
    length_all = tokens.shape[0] // groups

    def group_segments(lengths_row):
        return segment_ids(lengths_row, length_all)
    segments = jax.vmap(group_segments)(lengths)

    def forward(stream_in, gains, in_zx, in_bc, in_dt, kernel_x, kernel_bc, log_rates, step_bias, skip_gain, out_gain, out_weight):

        def per_group(group_items):
            stream, group_seg = group_items
            for layer_index in range(LAYERS):
                stream = layer_group(stream, group_seg, gains[layer_index], in_zx[layer_index], in_bc[layer_index], in_dt[layer_index], kernel_x[layer_index], kernel_bc[layer_index], log_rates[layer_index], step_bias[layer_index], skip_gain[layer_index], out_gain[layer_index], out_weight[layer_index])
            return stream
        grouped = lax.map(jax.checkpoint(per_group), (stream_in.reshape(groups, length_all, D), segments))
        return grouped.reshape(groups * length_all, D)
    outputs, pullback = jax.vjp(forward, tokens.astype(jnp.float32), norm_gain.astype(jnp.float32), w_zx.astype(jnp.float32), w_bc.astype(jnp.float32), w_dt.astype(jnp.float32), conv_x.astype(jnp.float32), conv_bc.astype(jnp.float32), a_log.astype(jnp.float32), dt_bias.astype(jnp.float32), d_skip.astype(jnp.float32), gate_gain.astype(jnp.float32), w_out.astype(jnp.float32))
    gradients = pullback(cotangent.astype(jnp.float32))
    return (outputs.astype(jnp.bfloat16), gradients[0], gradients[1], gradients[2], gradients[3], gradients[4], gradients[5], gradients[6], gradients[7], gradients[8], gradients[9], gradients[10], gradients[11])
```

```python
import functools

import jax
import jax.numpy as jnp
from jax import lax
from jax.experimental import pallas as pl
from jax.experimental.pallas import tpu as pltpu
from jax.sharding import PartitionSpec as P

D = 768
HEADS = 24
DI = 1536
LOCAL = 6
UNITS = 384
CONV = 640
TOK = 512
OWN = 128
HALF = 64
ROWS = 24
PAIR = 48
WIDE = 1536
HALFW = 768
MESH = pl.DeviceIdType.MESH
epsilon = 1e-05
highest = lax.Precision.HIGHEST
f32 = jnp.float32
bf16 = jnp.bfloat16
FAR = -1e30


def nn(a, b, precision=None):
    return lax.dot_general(
        a, b, (((1,), (0,)), ((), ())), precision=precision, preferred_element_type=f32
    )


def nt(a, b, precision=None):
    return lax.dot_general(
        a, b, (((1,), (1,)), ((), ())), precision=precision, preferred_element_type=f32
    )


def tn(a, b, precision=None):
    return lax.dot_general(
        a, b, (((0,), (0,)), ((), ())), precision=precision, preferred_element_type=f32
    )


def iota(shape, dim):
    return lax.broadcasted_iota(jnp.int32, shape, dim)


def softplus(v):
    return jnp.maximum(v, 0.0) + jnp.log1p(jnp.exp(-jnp.abs(v)))


def one_hot(condition, kind=f32):
    return jnp.where(condition, 1.0, 0.0).astype(kind)


def head_spread():
    return one_hot((iota((128, UNITS), 1) >> 6) == iota((128, UNITS), 0))


def to_row(column):
    eye = iota((128, 128), 0) == iota((128, 128), 1)
    return jnp.sum(jnp.where(eye, column, 0.0), axis=0, keepdims=True)


def to_column(row):
    eye = iota((128, 128), 0) == iota((128, 128), 1)
    return jnp.sum(jnp.where(eye, row, 0.0), axis=1, keepdims=True)


def small_lanes(tap, width, first):
    unit = iota((width, 128), 0)
    lane = iota((width, 128), 1)
    if width == UNITS:
        place = 6 + first + tap * 12 + (unit >> 6) * 2 + (unit & 1)
    else:
        place = 6 + first + tap * 8 + (unit & 7)
    return one_hot(lane == place, bf16)


def small_owner(width):
    unit = iota((32, width), 1)
    owner = (unit & 63) >> 1 if width == UNITS else unit >> 3
    return one_hot(owner == iota((32, width), 0))


SMALLS = (
    [(tap, UNITS, 0, tap, 0) for tap in range(5)]
    + [(tap, 256, 60, tap, UNITS) for tap in range(5)]
    + [(0, UNITS, 100, 5, 0)]
)


def placing():
    return one_hot(iota((D, 32), 0) == iota((D, 32), 1) * ROWS, bf16)


def forward_kernel(
    ng, weights, marks, segr, heads, proj, kept_y, logs, smalls, up, squares, bias, inner, act, xs
):
    proj[...] = nn(ng[...], weights[:, :1152])
    packed = tn(placing(), weights[:, 1024:1152]).astype(bf16)
    smalls[...] = jnp.zeros(smalls.shape, f32)
    for tap, width, first, row, start in SMALLS:
        spread = nt(packed, small_lanes(tap, width, first)) * small_owner(width)
        smalls[row : row + 1, start : start + width] = jnp.sum(spread, axis=0, keepdims=True)
    for ib in range(4):
        rows = slice(ib * 128, ib * 128 + 128)
        linked = (marks[rows, 3:4] == segr[0:1, :]) & (
            iota((128, TOK), 0) + ib * 128 >= iota((128, TOK), 1)
        )
        bias[rows, :] = jnp.where(linked, 0.0, FAR)
    lane = iota((TOK, 128), 1)
    steps = jnp.where(lane < LOCAL, softplus(proj[:, 1024:1152] + heads[0:1, :]), 0.0)
    rates = jnp.where(iota((1, 128), 1) < LOCAL, -jnp.exp(heads[1:2, :]), 0.0)
    log_now = nn(jnp.where(bias[...] == 0.0, 1.0, 0.0), steps * rates, highest)
    logs[...] = log_now
    log_t = log_now.T
    for c in range(0, CONV, 128):
        cols = slice(c, c + 128)
        v = proj[:, UNITS + c : UNITS + c + 128]
        y = smalls[4:5, cols] + smalls[3:4, cols] * v
        for s in (1, 2, 3):
            y = y + smalls[3 - s : 4 - s, cols] * (marks[:, s - 1 : s] * pltpu.roll(v, s, 0))
        act[:, cols] = (y * jax.nn.sigmoid(y)).astype(bf16)
    spread_heads = head_spread()
    skip_row = nn(heads[...], spread_heads, highest)[2:3, :]
    xs[...] = (act[:, :UNITS].astype(f32) * nn(steps, spread_heads, highest)).astype(bf16)
    inner[...] = nt(act[:, 512:640], act[:, 384:512])
    for ib in range(4):
        rows = slice(ib * 128, ib * 128 + 128)
        n = ib * 128 + 128
        for p in range(3):
            outs = []
            for h in (2 * p, 2 * p + 1):
                spread = log_now[rows, h : h + 1] - log_t[h : h + 1, :n] + bias[rows, :n]
                g = (inner[rows, :n] * jnp.exp(spread)).astype(bf16)
                outs.append(nn(g, xs[:n, p * 128 : p * 128 + 128]))
            kept_y[rows, p * 128 : p * 128 + 128] = jnp.where(
                iota((128, 128), 1) < 64, outs[0], outs[1]
            )
    total = jnp.zeros((8, TOK), f32)
    for p in range(3):
        cols = slice(p * 128, p * 128 + 128)
        gate = proj[:, cols]
        scanned = kept_y[:, cols] + skip_row[:, cols] * act[:, cols].astype(f32)
        gated = scanned * (gate * jax.nn.sigmoid(gate))
        total = total + nt(jnp.ones((8, 128), f32), gated * gated, highest)
        xs[:, cols] = (gated * smalls[5:6, cols]).astype(bf16)
    squares[...] = total
    up[...] = nt(xs[...], weights[:, 1152:]).astype(bf16)


def backward_kernel(
    gb,
    ng,
    weights,
    marks,
    segr,
    heads,
    proj,
    kept_y,
    logs,
    smalls,
    rk,
    gn,
    gw,
    head_out,
    bias,
    inner,
    dinner,
    act,
    xs,
    d16,
    mixed,
    z,
    dsc,
    grads,
    grad_small,
):
    for jb in range(4):
        rows = slice(jb * 128, jb * 128 + 128)
        linked = (marks[rows, 3:4] == segr[0:1, :]) & (
            iota((128, TOK), 0) + jb * 128 <= iota((128, TOK), 1)
        )
        bias[rows, :] = jnp.where(linked, 0.0, FAR)
    lane = iota((TOK, 128), 1)
    step_in = proj[:, 1024:1152] + heads[0:1, :]
    steps = jnp.where(lane < LOCAL, softplus(step_in), 0.0)
    rates = jnp.where(iota((1, 128), 1) < LOCAL, -jnp.exp(heads[1:2, :]), 0.0)
    log_now = logs[...]
    log_t = log_now.T
    spread_heads = head_spread()
    skip_row = nn(heads[...], spread_heads, highest)[2:3, :]
    step_wide = nn(steps, spread_heads, highest)

    def conv_of(c):
        cols = slice(c, c + 128)
        v = proj[:, UNITS + c : UNITS + c + 128]
        y = smalls[4:5, cols] + smalls[3:4, cols] * v
        for s in (1, 2, 3):
            y = y + smalls[3 - s : 4 - s, cols] * (marks[:, s - 1 : s] * pltpu.roll(v, s, 0))
        return v, y

    for c in range(0, CONV, 128):
        v, y = conv_of(c)
        act[:, c : c + 128] = (y * jax.nn.sigmoid(y)).astype(bf16)
    xs[...] = (act[:, :UNITS].astype(f32) * step_wide).astype(bf16)
    r = jnp.concatenate([to_column(rk[b, 0:1, :]) for b in range(4)], axis=0)
    k = jnp.concatenate([to_column(rk[b, 1:2, :]) for b in range(4)], axis=0)
    z[...] = nn(gb[...], weights[:, 1152:])
    head_rows = jnp.zeros((8, 128), f32)
    grad_small[...] = jnp.zeros(grad_small.shape, f32)
    skip_parts = []
    for p in range(3):
        cols = slice(p * 128, p * 128 + 128)
        gate = proj[:, cols]
        sig = jax.nn.sigmoid(gate)
        x = act[:, cols].astype(f32)
        scanned = kept_y[:, cols] + skip_row[:, cols] * x
        gated = scanned * (gate * sig)
        gain = smalls[5:6, cols]
        gm = z[:, cols]
        scaled = gated * r
        mixed[:, cols] = (scaled * gain).astype(bf16)
        grad_small[5:6, cols] = jnp.sum(gm * scaled, axis=0, keepdims=True)
        gg = r * (gm * gain) - gated * k
        ds_now = gg * (gate * sig)
        grads[:, cols] = (gg * scanned * sig * (1.0 + gate * (1.0 - sig))).astype(bf16)
        dsc[:, cols] = ds_now
        d16[:, cols] = ds_now.astype(bf16)
        skip_parts.append(jnp.sum(ds_now * x, axis=0, keepdims=True))
    gw[:, 1152:] = tn(gb[...], mixed[...]).astype(bf16)
    inner[...] = nt(act[:, 384:512], act[:, 512:640])
    dinner[...] = jnp.zeros(dinner.shape, f32)
    low_lanes = iota((128, 128), 1) < 64
    for jb in range(4):
        i0 = jb * 128
        rows = slice(i0, i0 + 128)
        for p in range(3):
            cols = slice(p * 128, p * 128 + 128)
            outs = []
            xp = xs[rows, cols]
            dp = d16[i0:, cols]
            for h in (2 * p, 2 * p + 1):
                spread = log_t[h : h + 1, i0:] - log_now[rows, h : h + 1] + bias[rows, i0:]
                e = jnp.exp(spread)
                outs.append(nn((inner[rows, i0:] * e).astype(bf16), dp))
                keep = low_lanes if h == 2 * p else jnp.logical_not(low_lanes)
                xh = jnp.where(keep, xp.astype(f32), 0.0).astype(bf16)
                dinner[rows, i0:] = dinner[rows, i0:] + e * nt(xh, dp)
            z[rows, cols] = jnp.where(low_lanes, outs[0], outs[1])
    x32 = act[:, :UNITS].astype(f32)
    zz = z[...]
    dlog = nt(d16[...].astype(f32) * kept_y[...] - xs[...].astype(f32) * zz, spread_heads, highest)
    dstep = nt(x32 * zz, spread_heads, highest)
    da = nn(jnp.where(bias[...] == 0.0, 1.0, 0.0), dlog, highest)
    dstep = dstep + da * rates
    ddt = jnp.where(lane < LOCAL, dstep * jax.nn.sigmoid(step_in), 0.0)
    skip_all = jnp.concatenate(skip_parts, axis=1)
    skip_heads = nt(jnp.broadcast_to(skip_all, (8, UNITS)), spread_heads, highest)
    row = iota((8, 128), 0)
    a_row = jnp.sum(da * steps, axis=0, keepdims=True) * rates
    b_row = jnp.sum(ddt, axis=0, keepdims=True)
    head_out[...] = jnp.where(
        row == 0, a_row, jnp.where(row == 1, b_row, jnp.where(row == 2, skip_heads, 0.0))
    )
    grads[:, 1024:1152] = ddt.astype(bf16)
    din = dinner[...].astype(bf16)
    grad_b = nn(din, act[:, 512:640])
    grad_c = tn(din, act[:, 384:512])
    for c in range(0, CONV, 128):
        cols = slice(c, c + 128)
        if c < UNITS:
            dact = step_wide[:, cols] * z[:, cols] + skip_row[:, cols] * dsc[:, cols]
        else:
            dact = grad_b if c == UNITS else grad_c
        v, y = conv_of(c)
        sig = jax.nn.sigmoid(y)
        dy = dact * sig * (1.0 + y * (1.0 - sig))
        grad_small[4:5, cols] = jnp.sum(dy, axis=0, keepdims=True)
        grad_small[3:4, cols] = jnp.sum(dy * v, axis=0, keepdims=True)
        dv = smalls[3:4, cols] * dy
        for s in (1, 2, 3):
            masked = marks[:, s - 1 : s] * dy
            grad_small[3 - s : 4 - s, cols] = jnp.sum(
                masked * pltpu.roll(v, s, 0), axis=0, keepdims=True
            )
            dv = dv + smalls[3 - s : 4 - s, cols] * pltpu.roll(masked, TOK - s, 0)
        grads[:, UNITS + c : UNITS + c + 128] = dv.astype(bf16)
    gn[...] = nt(grads[...], weights[:, :1152]).astype(bf16)
    gw[:, :1024] = tn(ng[...], grads[:, :1024]).astype(bf16)
    packed = jnp.zeros((32, 128), f32)
    for tap, width, first, row_at, start in SMALLS:
        values = (
            small_owner(width) * grad_small[row_at : row_at + 1, start : start + width]
        ).astype(bf16)
        packed = packed + nn(values, small_lanes(tap, width, first))
    last = tn(ng[...], grads[:, 1024:1152]) + nn(placing(), packed.astype(bf16))
    gw[:, 1024:1152] = last.astype(bf16)


VM = pl.BlockSpec(memory_space=pltpu.VMEM)


def compute_call(kernel, out_shape, scratch, args):
    return pl.pallas_call(
        kernel,
        out_shape=out_shape,
        in_specs=[VM] * len(args),
        out_specs=[VM] * len(out_shape),
        scratch_shapes=scratch,
        compiler_params=pltpu.CompilerParams(vmem_limit_bytes=56 * 1024 * 1024),
    )(*args)


def shaped(shape, kind=f32):
    return jax.ShapeDtypeStruct(shape, kind)


def forward_call(ng, weights, marks, segr, heads):
    return compute_call(
        forward_kernel,
        [
            shaped((TOK, 1152)),
            shaped((TOK, UNITS)),
            shaped((TOK, 128)),
            shaped((8, CONV)),
            shaped((TOK, D), bf16),
            shaped((8, TOK)),
        ],
        [
            pltpu.VMEM((TOK, TOK), f32),
            pltpu.VMEM((TOK, TOK), f32),
            pltpu.VMEM((TOK, CONV), bf16),
            pltpu.VMEM((TOK, UNITS), bf16),
        ],
        (ng, weights, marks, segr, heads),
    )


def backward_call(*args):
    return compute_call(
        backward_kernel,
        [shaped((TOK, D), bf16), shaped((D, WIDE), bf16), shaped((8, 128))],
        [
            pltpu.VMEM((TOK, TOK), f32),
            pltpu.VMEM((TOK, TOK), f32),
            pltpu.VMEM((TOK, TOK), f32),
            pltpu.VMEM((TOK, CONV), bf16),
            pltpu.VMEM((TOK, UNITS), bf16),
            pltpu.VMEM((TOK, UNITS), bf16),
            pltpu.VMEM((TOK, UNITS), bf16),
            pltpu.VMEM((TOK, UNITS), f32),
            pltpu.VMEM((TOK, UNITS), f32),
            pltpu.VMEM((TOK, 1152), bf16),
            pltpu.VMEM((8, CONV), f32),
        ],
        args,
    )


def marks_of(pieces):
    endings = jnp.cumsum(pieces)
    places = jnp.arange(TOK, dtype=jnp.int32)
    segment = jnp.sum((places[:, None] >= endings[None, :]).astype(jnp.int32), axis=1)
    starts = jnp.max(
        jnp.where(places[:, None] >= endings[None, :], endings[None, :], 0), axis=1
    )
    since = places - starts
    lane = jnp.arange(128, dtype=jnp.int32)[None, :]
    marks = jnp.where(
        lane < 3, (since[:, None] > lane).astype(f32), segment[:, None].astype(f32)
    )
    return marks, jnp.broadcast_to(segment.astype(f32)[None, :], (8, TOK))


class Place:
    def __init__(self):
        self.dp = lax.axis_index("dp")
        self.x = lax.axis_index("tensor")
        self.core = self.dp % 2
        self.other = 1 - self.core
        self.chip = self.dp // 2
        y, z = self.chip % 4, self.chip // 4
        self.a = self.other * y + self.core * z
        self.b = self.other * z + self.core * y
        self.partner = (self.chip * 2 + self.other, self.x)
        self.right = (self.dp, (self.x + 1) % 4)
        self.left = (self.dp, (self.x + 3) % 4)

    def chip_at(self, a, b):
        return self.other * (b * 4 + a) + self.core * (a * 4 + b)

    def partners_chip_at(self, a, b):
        return self.core * (b * 4 + a) + self.other * (a * 4 + b)

    def along_a(self, k):
        return (self.chip_at((self.a + k) % 4, self.b) * 2 + self.core, self.x)

    def along_b(self, k):
        return (self.chip_at(self.a, (self.b + k) % 4) * 2 + self.core, self.x)

    def along_x(self, k):
        return (self.dp, (self.x + k) % 4)


def greet(peers):
    barrier = pltpu.get_barrier_semaphore()
    for peer in peers:
        pl.semaphore_signal(barrier, inc=1, device_id=peer, device_id_type=MESH)
    pl.semaphore_wait(barrier, len(peers))


def x_peers(at):
    return [at.along_x(k) for k in (1, 2, 3)]


def all_peers(at):
    return (
        [at.partner]
        + [at.along_a(k) for k in (1, 2, 3)]
        + [at.along_b(k) for k in (1, 2, 3)]
        + x_peers(at)
    )


class Sems:
    def __init__(self, send, recv):
        self.send, self.recv, self.used = send, recv, 0

    def copy(self, src, dst, device):
        index = self.used
        self.used += 1
        made = pltpu.make_async_remote_copy(
            src_ref=src,
            dst_ref=dst,
            send_sem=self.send.at[index],
            recv_sem=self.recv.at[index],
            device_id=device,
            device_id_type=MESH,
        )
        made.start()
        return made


def together(*parts):
    parts = list(parts)
    while parts:
        for part in list(parts):
            try:
                next(part)
            except StopIteration:
                parts.remove(part)


def rows_of(start, count, multiple):
    return pl.ds(pl.multiple_of(start, multiple), count)


def half_rows(block, half):
    return rows_of(block * OWN + half * HALF, HALF, HALF)


def gather_x(at, sems, out):
    def block(b, half):
        return out.at[half_rows(b, half), :]

    x, r, l = at.x, (at.x + 1) % 4, (at.x + 3) % 4
    c0 = sems.copy(block(x, 0), block(x, 0), at.right)
    c1 = sems.copy(block(x, 1), block(x, 1), at.left)
    c2 = sems.copy(block(x, 1), block(x, 1), at.right)
    c3 = sems.copy(block(x, 0), block(x, 0), at.left)
    yield
    c0.wait_recv()
    c4 = sems.copy(block(l, 0), block(l, 0), at.right)
    yield
    c1.wait_recv()
    c5 = sems.copy(block(r, 1), block(r, 1), at.left)
    yield
    for c in (c2, c3, c4, c5):
        c.wait_recv()
    for c in (c0, c1, c2, c3, c4, c5):
        c.wait_send()


def scatter_x(at, sems, up, buf, tmp, total):
    def block(b, half):
        return up.at[half_rows(b, half), :]

    def value(b, half):
        return up[half_rows(b, half), :].astype(f32)

    x, r, l, o = at.x, (at.x + 1) % 4, (at.x + 3) % 4, (at.x + 2) % 4
    c0 = sems.copy(block(o, 0), buf.at[0], at.right)
    c1 = sems.copy(block(o, 1), buf.at[1], at.left)
    c2 = sems.copy(block(r, 1), buf.at[2], at.right)
    c3 = sems.copy(block(l, 0), buf.at[3], at.left)
    yield
    c0.wait_recv()
    tmp[0] = (value(r, 0) + buf[0].astype(f32)).astype(bf16)
    c4 = sems.copy(tmp.at[0], buf.at[4], at.right)
    yield
    c1.wait_recv()
    tmp[1] = (value(l, 1) + buf[1].astype(f32)).astype(bf16)
    c5 = sems.copy(tmp.at[1], buf.at[5], at.left)
    yield
    for c in (c2, c3, c4, c5):
        c.wait_recv()
    total[0:HALF, :] = value(x, 0) + buf[4].astype(f32) + buf[3].astype(f32)
    total[HALF:OWN, :] = value(x, 1) + buf[2].astype(f32) + buf[5].astype(f32)
    for c in (c0, c1, c2, c3, c4, c5):
        c.wait_send()


def share_squares(at, sems, squares, buf):
    def lanes(x):
        return rows_of(x * OWN, OWN, OWN)

    copies = [
        sems.copy(squares.at[:, lanes((at.x + k) % 4)], buf.at[k - 1], at.along_x(k))
        for k in (1, 2, 3)
    ]
    yield
    for c in copies:
        c.wait_recv()
    buf[3] = squares[:, lanes(at.x)] + buf[0] + buf[1] + buf[2]
    for c in copies:
        c.wait_send()


def share_rows(at, sems, rk):
    copies = [sems.copy(rk.at[at.x], rk.at[at.x], at.along_x(k)) for k in (1, 2, 3)]
    yield
    for c in copies:
        c.wait_recv()
    for c in copies:
        c.wait_send()


def gather_weights(at, sems, shard, met, out):
    mine = rows_of(at.core * HALFW, HALFW, HALFW)

    def block(chip):
        return out.at[rows_of(chip * PAIR, PAIR, PAIR), mine]

    first = sems.copy(shard, met, at.partner)
    yield
    first.wait_recv()
    core = at.core.astype(f32)
    own, theirs = shard[0:ROWS, :].astype(f32), met[0:ROWS, :].astype(f32)
    low = own * (1.0 - core) + theirs * core
    high = own * core + theirs * (1.0 - core)
    out[rows_of(at.chip * PAIR, PAIR, PAIR), :] = jnp.concatenate([low, high], axis=0).astype(bf16)
    along_a = [None] + [sems.copy(block(at.chip), block(at.chip), at.along_a(k)) for k in (1, 2, 3)]
    along_b = []
    passed = []
    for k in range(4):
        if k:
            yield
            along_a[k].wait_recv()
        now = block(at.chip_at((at.a + 4 - k) % 4, at.b))
        for j in (1, 2, 3):
            along_b.append((k, j, sems.copy(now, now, at.along_b(j))))
        if k:
            passed.append(sems.copy(now, now, at.partner))
    for k, j, c in along_b:
        yield
        c.wait_recv()
        now = block(at.chip_at((at.a + 4 - k) % 4, (at.b + 4 - j) % 4))
        passed.append(sems.copy(now, now, at.partner))
    yield
    for c in passed:
        c.wait_recv()
    for c in [first] + along_a[1:] + [c for _, _, c in along_b] + passed:
        c.wait_send()


def scatter_weights(at, sems, grads, out, met, held, got, sums, got_last, final, met_final, xsend, xgot):
    mine = rows_of(at.core * HALFW, HALFW, HALFW)
    others = rows_of(at.other * HALFW, HALFW, HALFW)

    def rows(chip):
        return rows_of(chip * PAIR, PAIR, PAIR)

    order = [(j, m) for j in (1, 2, 3, 0) for m in range(4)]
    first = []
    for j, m in order:
        chip = at.partners_chip_at(m, (at.a + j) % 4)
        first.append(sems.copy(grads.at[rows(chip), others], met.at[rows(chip), :], at.partner))
    second = []
    for (j, m), c in zip(order, first):
        if m == 0:
            yield
        c.wait_recv()
        chip = at.chip_at(m, (at.b + j) % 4)
        both = grads[rows(chip), mine].astype(f32) + met[rows(chip), :].astype(f32)
        held[j, m] = both.astype(bf16)
        if j:
            second.append(sems.copy(held.at[j, m], got.at[j - 1, m], at.along_b(j)))
    yield
    for c in second:
        c.wait_recv()

    def summed(m):
        return (
            held[0, m].astype(f32)
            + got[0, m].astype(f32)
            + got[1, m].astype(f32)
            + got[2, m].astype(f32)
        )

    third = []
    for k in (1, 2, 3):
        sums[k] = summed((at.a + k) % 4).astype(bf16)
        third.append(sems.copy(sums.at[k], got_last.at[k - 1], at.along_a(k)))
    last = summed(at.a)
    yield
    for c in third:
        c.wait_recv()
    final[...] = (
        last
        + got_last[0].astype(f32)
        + got_last[1].astype(f32)
        + got_last[2].astype(f32)
    )
    fourth = sems.copy(final.at[rows_of(at.other * ROWS, ROWS, 8), :], met_final, at.partner)
    out[:, mine] = final[rows_of(at.core * ROWS, ROWS, 8), :]
    yield
    fourth.wait_recv()
    out[:, others] = met_final[...]
    xsend[...] = out[:, 768:1152]
    fifth = [sems.copy(xsend, xgot.at[k - 1], at.along_x(k)) for k in (1, 2, 3)]
    yield
    for c in fifth:
        c.wait_recv()
    lane = iota((ROWS, 384), 1)
    shared = (lane < 256) | ((lane >= 256 + 66) & (lane < 256 + 106))
    out[:, 768:1152] = xsend[...] + jnp.where(shared, xgot[0] + xgot[1] + xgot[2], 0.0)
    for c in first + second + third + [fourth] + fifth:
        c.wait_send()


def sum_everywhere(at, sems, values, held, got):
    held[0] = values[...]
    slot = 0
    stages = [
        [at.partner],
        [at.along_a(k) for k in (1, 2, 3)],
        [at.along_b(k) for k in (1, 2, 3)],
        [at.along_x(k) for k in (1, 2, 3)],
    ]
    for stage, peers in enumerate(stages):
        copies = []
        for peer in peers:
            copies.append(sems.copy(held.at[stage], got.at[slot], peer))
            slot += 1
        yield
        for c in copies:
            c.wait_recv()
        more = got[slot - len(peers)]
        for s in range(slot - len(peers) + 1, slot):
            more = more + got[s]
        if stage == 3:
            more = jnp.where(iota((32, 128), 0) < 16, more, 0.0)
        held[stage + 1] = held[stage] + more
        for c in copies:
            c.wait_send()
    values[...] = held[4]


def row_scale(values):
    return lax.rsqrt(jnp.mean(values * values, axis=-1, keepdims=True) + epsilon)


def put_own(at, out, values):
    out[rows_of(at.x * OWN, OWN, OWN), :] = values


def put_rows(at, rk, r, k):
    row = iota((8, 128), 0)
    rk[at.x] = jnp.where(row == 0, to_row(r), jnp.where(row == 1, to_row(k), 0.0))


def start_kernel(shard, tokens, gains, cot, weights, ng, gb, met, send, recv):
    at = Place()
    sems = Sems(send, recv)
    greet(all_peers(at))
    moving = gather_weights(at, sems, shard, met, weights)
    next(moving)
    stream = tokens[...].astype(f32)
    put_own(at, ng, (stream * row_scale(stream) * gains[0:1, :]).astype(bf16))
    put_own(at, gb, cot[...])
    together(moving, gather_x(at, sems, ng), gather_x(at, sems, gb))


def gate_scale(sqbuf):
    return to_column(lax.rsqrt(sqbuf[3][0:1, :] / DI + epsilon))


def middle_kernel(
    up, squares, tokens, gains, shard, stream1, branch0, r0, ng, weights,
    met, buf, tmp, total, sqbuf, send, recv,
):
    at = Place()
    sems = Sems(send, recv)
    greet(all_peers(at))
    moving = gather_weights(at, sems, shard, met, weights)

    def along():
        yield from scatter_x(at, sems, up, buf, tmp, total)
        r = gate_scale(sqbuf)
        branch = r * total[...]
        stream = tokens[...].astype(f32) + branch
        branch0[...] = branch
        stream1[...] = stream
        r0[...] = jnp.broadcast_to(to_row(r), (8, 128))
        put_own(at, ng, (stream * row_scale(stream) * gains[1:2, :]).astype(bf16))
        yield from gather_x(at, sems, ng)

    together(share_squares(at, sems, squares, sqbuf), along(), moving)


def turn_kernel(
    up, squares, stream1, cot, block_out, rk, buf, tmp, total, sqbuf, send, recv
):
    at = Place()
    sems = Sems(send, recv)
    greet(x_peers(at))
    together(share_squares(at, sems, squares, sqbuf), scatter_x(at, sems, up, buf, tmp, total))
    r = gate_scale(sqbuf)
    branch = r * total[...]
    block_out[...] = (stream1[...] + branch).astype(bf16)
    dots = jnp.sum(cot[...].astype(f32) * branch, axis=1, keepdims=True)
    put_rows(at, rk, r, r * r * dots / DI)
    together(share_rows(at, sems, rk))


def norm_back(gnorm, stream, gain, grad):
    q = row_scale(stream)
    gain_row = jnp.sum(gnorm * stream * q, axis=0, keepdims=True)
    rows = gnorm * gain
    inner = jnp.mean(rows * stream, axis=1, keepdims=True)
    return grad + q * rows - stream * (q * q * q) * inner, gain_row


def back_kernel(
    gn, stream1, gains, cot, branch0, r0, gw, grad0, gb, rk, gg, out,
    buf, tmp, total, *rest,
):
    at = Place()
    sems = Sems(*rest[-2:])
    greet(all_peers(at))

    def along():
        yield from scatter_x(at, sems, gn, buf, tmp, total)
        grad, gain_row = norm_back(
            total[...], stream1[...], gains[1:2, :], cot[...].astype(f32)
        )
        low = grad.astype(bf16)
        put_own(at, gb, low)
        sharing = gather_x(at, sems, gb)
        next(sharing)
        grad0[...] = grad
        r = to_column(r0[0:1, :])
        dots = jnp.sum(low.astype(f32) * branch0[...], axis=1, keepdims=True)
        put_rows(at, rk, r, r * r * dots / DI)
        rows = share_rows(at, sems, rk)
        next(rows)
        gg[...] = jnp.zeros(gg.shape, f32)
        for c in range(6):
            gg[c : c + 1, :] = gain_row[:, c * 128 : c * 128 + 128]
        yield from sharing
        yield from rows

    together(along(), scatter_weights(at, sems, gw, out, *rest[:-2]))


def end_kernel(
    gn, tokens, gains, grad0, gw, gg1, head0, head1, input_grad, out, values,
    buf, tmp, total, held, got, *rest,
):
    at = Place()
    sems = Sems(*rest[-2:])
    greet(all_peers(at))

    def along():
        yield from scatter_x(at, sems, gn, buf, tmp, total)
        grad, gain_row = norm_back(
            total[...], tokens[...].astype(f32), gains[0:1, :], grad0[...]
        )
        input_grad[...] = grad
        values[...] = jnp.zeros(values.shape, f32)
        for c in range(6):
            values[c : c + 1, :] = gain_row[:, c * 128 : c * 128 + 128]
        values[6:12, :] = gg1[0:6, :]
        values[16:24, :] = head0[...]
        values[24:32, :] = head1[...]
        yield from sum_everywhere(at, sems, values, held, got)

    together(along(), scatter_weights(at, sems, gw, out, *rest[:-2]))


def send_call(kernel, number, copies, out_shape, scratch, args):
    return pl.pallas_call(
        kernel,
        out_shape=out_shape,
        in_specs=[VM] * len(args),
        out_specs=[VM] * len(out_shape),
        scratch_shapes=scratch
        + [pltpu.SemaphoreType.DMA((copies,)), pltpu.SemaphoreType.DMA((copies,))],
        compiler_params=pltpu.CompilerParams(
            collective_id=number, has_side_effects=True, vmem_limit_bytes=56 * 1024 * 1024
        ),
    )(*args)


RING = [
    pltpu.VMEM((6, HALF, D), bf16),
    pltpu.VMEM((2, HALF, D), bf16),
    pltpu.VMEM((OWN, D), f32),
]
SCATTER = [
    pltpu.VMEM((D, HALFW), bf16),
    pltpu.VMEM((4, 4, PAIR, HALFW), bf16),
    pltpu.VMEM((3, 4, PAIR, HALFW), bf16),
    pltpu.VMEM((4, PAIR, HALFW), bf16),
    pltpu.VMEM((3, PAIR, HALFW), bf16),
    pltpu.VMEM((PAIR, HALFW), f32),
    pltpu.VMEM((ROWS, HALFW), f32),
    pltpu.VMEM((ROWS, 384), f32),
    pltpu.VMEM((3, ROWS, 384), f32),
]


def pack_layer(w_zx, w_bc, w_dt, conv_x, conv_bc, gate_gain, w_out):
    small = jnp.concatenate([conv_x.reshape(-1), conv_bc.reshape(-1), gate_gain.reshape(-1)])
    steps = jnp.concatenate(
        [w_dt, jnp.pad(small[None, :], ((0, ROWS - 1), (0, 128 - LOCAL - small.shape[0])))], axis=1
    )
    packed = jnp.concatenate([w_zx.reshape(ROWS, 768), w_bc, steps, w_out.T], axis=1)
    return jnp.pad(packed, ((0, 32 - ROWS), (0, 0)))


def body(
    tokens,
    lengths,
    norm_gain,
    w_zx,
    w_bc,
    w_dt,
    conv_x,
    conv_bc,
    a_log,
    dt_bias,
    d_skip,
    gate_gain,
    w_out,
    cotangent,
):
    marks, segr = marks_of(lengths[0])
    shards = [
        pack_layer(w_zx[l], w_bc[l], w_dt[l], conv_x[l], conv_bc[l], gate_gain[l], w_out[l])
        for l in range(2)
    ]
    heads = [
        jnp.pad(jnp.stack([dt_bias[l], a_log[l], d_skip[l]]), ((0, 5), (0, 128 - LOCAL)))
        for l in range(2)
    ]
    weights0, ng0, gb1 = send_call(
        start_kernel,
        0,
        43,
        [shaped((D, WIDE), bf16), shaped((TOK, D), bf16), shaped((TOK, D), bf16)],
        [pltpu.VMEM((32, WIDE), bf16)],
        (shards[0], tokens, norm_gain, cotangent),
    )
    proj0, y0, logs0, small0, up0, squares0 = forward_call(ng0, weights0, marks, segr, heads[0])
    stream1, branch0, r0, ng1, weights1 = send_call(
        middle_kernel,
        1,
        46,
        [
            shaped((OWN, D)),
            shaped((OWN, D)),
            shaped((8, 128)),
            shaped((TOK, D), bf16),
            shaped((D, WIDE), bf16),
        ],
        [pltpu.VMEM((32, WIDE), bf16)] + RING + [pltpu.VMEM((4, 8, 128), f32)],
        (up0, squares0, tokens, norm_gain, shards[1]),
    )
    proj1, y1, logs1, small1, up1, squares1 = forward_call(ng1, weights1, marks, segr, heads[1])
    block_out, rk1 = send_call(
        turn_kernel,
        2,
        12,
        [shaped((OWN, D), bf16), shaped((4, 8, 128))],
        RING + [pltpu.VMEM((4, 8, 128), f32)],
        (up1, squares1, stream1, cotangent),
    )
    gn1, gw1, head1 = backward_call(
        gb1, ng1, weights1, marks, segr, heads[1], proj1, y1, logs1, small1, rk1
    )
    grad0, gb0, rk0, gg1, sum1 = send_call(
        back_kernel,
        3,
        50,
        [
            shaped((OWN, D)),
            shaped((TOK, D), bf16),
            shaped((4, 8, 128)),
            shaped((8, 128)),
            shaped((ROWS, WIDE)),
        ],
        RING + SCATTER,
        (gn1, stream1, norm_gain, cotangent, branch0, r0, gw1),
    )
    gn0, gw0, head0 = backward_call(
        gb0, ng0, weights0, marks, segr, heads[0], proj0, y0, logs0, small0, rk0
    )
    input_grad, sum0, values = send_call(
        end_kernel,
        4,
        51,
        [shaped((OWN, D)), shaped((ROWS, WIDE)), shaped((32, 128))],
        RING + [pltpu.VMEM((5, 32, 128), f32), pltpu.VMEM((10, 32, 128), f32)] + SCATTER,
        (gn0, tokens, norm_gain, grad0, gw0, gg1, head0, head1),
    )
    sums = jnp.stack([sum0, sum1])
    small = sums[:, 0, 1030:1142]
    head_grads = values[16:32, :].reshape(2, 8, 128)[:, :3, :LOCAL]
    return (
        block_out,
        input_grad,
        values[:12, :].reshape(2, D),
        sums[:, :, :768].reshape(2, ROWS, 2, UNITS),
        sums[:, :, 768:1024],
        sums[:, :, 1024:1030],
        small[:, :60].reshape(2, 5, LOCAL, 2),
        small[:, 60:100].reshape(2, 5, 8),
        head_grads[:, 0],
        head_grads[:, 1],
        head_grads[:, 2],
        small[:, 100:112].reshape(2, LOCAL, 2),
        jnp.swapaxes(sums[:, :, 1152:], 1, 2),
    )


def solution(mesh):
    return jax.shard_map(
        body,
        mesh=mesh,
        in_specs=(
            P(("dp", "tensor"), None),
            P("dp", None),
            P(),
            P(None, "dp", None, "tensor"),
            P(None, "dp", None),
            P(None, "dp", "tensor"),
            P(None, None, "tensor", "dp"),
            P(None, None, "dp"),
            P(None, "tensor"),
            P(None, "tensor"),
            P(None, "tensor"),
            P(None, "tensor", "dp"),
            P(None, "tensor", "dp"),
            P(("dp", "tensor"), None),
        ),
        out_specs=(
            P(("dp", "tensor"), None),
            P(("dp", "tensor"), None),
            P(),
            P(None, "dp", None, "tensor"),
            P(None, "dp", None),
            P(None, "dp", "tensor"),
            P(None, None, "tensor", "dp"),
            P(None, None, "dp"),
            P(None, "tensor"),
            P(None, "tensor"),
            P(None, "tensor"),
            P(None, "tensor", "dp"),
            P(None, "tensor", "dp"),
        ),
        check_vma=False,
    )
```

```python
import functools

import jax
import jax.numpy as jnp
from jax import lax
from jax.experimental import pallas as pl
from jax.experimental.pallas import tpu as pltpu
from jax.sharding import PartitionSpec as P

D = 768
HEADS = 24
DI = 1536
LOCAL = 6
UNITS = 384
CONV = 640
TOK = 512
OWN = 128
HALF = 64
ROWS = 24
PAIR = 48
WIDE = 1536
HALFW = 768
MESH = pl.DeviceIdType.MESH
epsilon = 1e-05
highest = lax.Precision.HIGHEST
f32 = jnp.float32
bf16 = jnp.bfloat16
FAR = -1e30


def nn(a, b, precision=None):
    return lax.dot_general(
        a, b, (((1,), (0,)), ((), ())), precision=precision, preferred_element_type=f32
    )


def nt(a, b, precision=None):
    return lax.dot_general(
        a, b, (((1,), (1,)), ((), ())), precision=precision, preferred_element_type=f32
    )


def tn(a, b, precision=None):
    return lax.dot_general(
        a, b, (((0,), (0,)), ((), ())), precision=precision, preferred_element_type=f32
    )


def iota(shape, dim):
    return lax.broadcasted_iota(jnp.int32, shape, dim)


def softplus(v):
    return jnp.maximum(v, 0.0) + jnp.log1p(jnp.exp(-jnp.abs(v)))


def one_hot(condition, kind=f32):
    return jnp.where(condition, 1.0, 0.0).astype(kind)


def head_spread():
    return one_hot((iota((128, UNITS), 1) >> 6) == iota((128, UNITS), 0))


def to_row(column):
    eye = iota((128, 128), 0) == iota((128, 128), 1)
    return jnp.sum(jnp.where(eye, column, 0.0), axis=0, keepdims=True)


def to_column(row):
    eye = iota((128, 128), 0) == iota((128, 128), 1)
    return jnp.sum(jnp.where(eye, row, 0.0), axis=1, keepdims=True)


def small_lanes(tap, width, first):
    unit = iota((width, 128), 0)
    lane = iota((width, 128), 1)
    if width == UNITS:
        place = 6 + first + tap * 12 + (unit & 1) * 6 + (unit >> 6)
    else:
        place = 6 + first + tap * 8 + (unit & 7)
    return one_hot(lane == place, bf16)


def small_owner(width):
    unit = iota((32, width), 1)
    owner = (unit & 63) >> 1 if width == UNITS else unit >> 3
    return one_hot(owner == iota((32, width), 0))


SMALLS = (
    [(tap, UNITS, 0, tap, 0) for tap in range(5)]
    + [(tap, 256, 60, tap, UNITS) for tap in range(5)]
    + [(0, UNITS, 100, 5, 0)]
)


def placing():
    return one_hot(iota((D, 32), 0) == iota((D, 32), 1) * ROWS, bf16)


def segment_starts(lengths, position):
    first = lengths[0, 0]
    second = first + lengths[0, 1]
    return jnp.where(position >= second, second, jnp.where(position >= first, first, 0))


def fill_marks(lengths, marks):
    position = iota((TOK, 128), 0)
    since = position - segment_starts(lengths, position)
    for s in (1, 2, 3):
        marks[s - 1] = one_hot(since >= s)


def fill_heads(layer, step_bias, log_rates, skips, heads):
    heads[...] = jnp.zeros(heads.shape, f32)
    for row, values in enumerate((step_bias, log_rates, skips)):
        heads[row : row + 1, 0:LOCAL] = values[layer : layer + 1, :]


def forward_steps(
    layer, ng, weights, lengths, step_bias, log_rates, skips,
    proj, kept_y, logs, smalls, up, squares,
    marks, heads, bias, inner, act, xs,
):
    fill_marks(lengths, marks)
    fill_heads(layer, step_bias, log_rates, skips, heads)
    proj[...] = nn(ng[...], weights[:, :1152])
    yield
    packed = tn(placing(), weights[:, 1024:1152]).astype(bf16)
    smalls[...] = jnp.zeros(smalls.shape, f32)
    for tap, width, first, row, start in SMALLS:
        spread = nt(packed, small_lanes(tap, width, first)) * small_owner(width)
        smalls[row : row + 1, start : start + width] = jnp.sum(spread, axis=0, keepdims=True)
    for ib in range(4):
        rows = slice(ib * 128, ib * 128 + 128)
        here, there = iota((128, TOK), 0) + ib * 128, iota((128, TOK), 1)
        linked = (there <= here) & (there >= segment_starts(lengths, here))
        bias[rows, :] = jnp.where(linked, 0.0, FAR)
    yield
    lane = iota((TOK, 128), 1)
    steps = jnp.where(lane < LOCAL, softplus(proj[:, 1024:1152] + heads[0:1, :]), 0.0)
    rates = jnp.where(iota((1, 128), 1) < LOCAL, -jnp.exp(heads[1:2, :]), 0.0)
    log_now = nn(jnp.where(bias[...] == 0.0, 1.0, 0.0), steps * rates, highest)
    logs[...] = log_now
    log_t = log_now.T
    for c in range(0, CONV, 128):
        cols = slice(c, c + 128)
        v = proj[:, UNITS + c : UNITS + c + 128]
        y = smalls[4:5, cols] + smalls[3:4, cols] * v
        for s in (1, 2, 3):
            y = y + smalls[3 - s : 4 - s, cols] * (marks[s - 1] * pltpu.roll(v, s, 0))
        act[:, cols] = (y * jax.nn.sigmoid(y)).astype(bf16)
    yield
    spread_heads = head_spread()
    skip_row = nn(heads[...], spread_heads, highest)[2:3, :]
    xs[...] = (act[:, :UNITS].astype(f32) * nn(steps, spread_heads, highest)).astype(bf16)
    inner[...] = nt(act[:, 512:640], act[:, 384:512])
    yield
    for ib in range(4):
        rows = slice(ib * 128, ib * 128 + 128)
        n = ib * 128 + 128
        for p in range(3):
            outs = []
            for h in (2 * p, 2 * p + 1):
                spread = log_now[rows, h : h + 1] - log_t[h : h + 1, :n] + bias[rows, :n]
                g = (inner[rows, :n] * jnp.exp(spread)).astype(bf16)
                outs.append(nn(g, xs[:n, p * 128 : p * 128 + 128]))
            kept_y[rows, p * 128 : p * 128 + 128] = jnp.where(
                iota((128, 128), 1) < 64, outs[0], outs[1]
            )
        yield
    total = jnp.zeros((8, TOK), f32)
    for p in range(3):
        cols = slice(p * 128, p * 128 + 128)
        gate = proj[:, cols]
        scanned = kept_y[:, cols] + skip_row[:, cols] * act[:, cols].astype(f32)
        gated = scanned * (gate * jax.nn.sigmoid(gate))
        total = total + nt(jnp.ones((8, 128), f32), gated * gated, highest)
        xs[:, cols] = (gated * smalls[5:6, cols]).astype(bf16)
    squares[...] = total
    up[...] = nt(xs[...], weights[:, 1152:]).astype(bf16)


def backward_steps(
    layer,
    gb,
    ng,
    weights,
    lengths,
    step_bias,
    log_rates,
    skips,
    proj,
    kept_y,
    logs,
    smalls,
    rk,
    gn,
    gw,
    head_out,
    marks,
    heads,
    bias,
    inner,
    dinner,
    act,
    xs,
    d16,
    mixed,
    z,
    dsc,
    grads,
    grad_small,
):
    fill_marks(lengths, marks)
    fill_heads(layer, step_bias, log_rates, skips, heads)
    for jb in range(4):
        rows = slice(jb * 128, jb * 128 + 128)
        here, there = iota((128, TOK), 0) + jb * 128, iota((128, TOK), 1)
        linked = (here <= there) & (here >= segment_starts(lengths, there))
        bias[rows, :] = jnp.where(linked, 0.0, FAR)
    lane = iota((TOK, 128), 1)
    step_in = proj[:, 1024:1152] + heads[0:1, :]
    steps = jnp.where(lane < LOCAL, softplus(step_in), 0.0)
    rates = jnp.where(iota((1, 128), 1) < LOCAL, -jnp.exp(heads[1:2, :]), 0.0)
    log_now = logs[...]
    log_t = log_now.T
    spread_heads = head_spread()
    skip_row = nn(heads[...], spread_heads, highest)[2:3, :]
    step_wide = nn(steps, spread_heads, highest)

    def conv_of(c):
        cols = slice(c, c + 128)
        v = proj[:, UNITS + c : UNITS + c + 128]
        y = smalls[4:5, cols] + smalls[3:4, cols] * v
        for s in (1, 2, 3):
            y = y + smalls[3 - s : 4 - s, cols] * (marks[s - 1] * pltpu.roll(v, s, 0))
        return v, y

    for c in range(0, CONV, 128):
        v, y = conv_of(c)
        act[:, c : c + 128] = (y * jax.nn.sigmoid(y)).astype(bf16)
    xs[...] = (act[:, :UNITS].astype(f32) * step_wide).astype(bf16)
    r = jnp.concatenate([to_column(rk[b, 0:1, :]) for b in range(4)], axis=0)
    k = jnp.concatenate([to_column(rk[b, 1:2, :]) for b in range(4)], axis=0)
    z[...] = nn(gb[...], weights[:, 1152:])
    head_rows = jnp.zeros((8, 128), f32)
    grad_small[...] = jnp.zeros(grad_small.shape, f32)
    skip_parts = []
    for p in range(3):
        cols = slice(p * 128, p * 128 + 128)
        gate = proj[:, cols]
        sig = jax.nn.sigmoid(gate)
        x = act[:, cols].astype(f32)
        scanned = kept_y[:, cols] + skip_row[:, cols] * x
        gated = scanned * (gate * sig)
        gain = smalls[5:6, cols]
        gm = z[:, cols]
        scaled = gated * r
        mixed[:, cols] = (scaled * gain).astype(bf16)
        grad_small[5:6, cols] = jnp.sum(gm * scaled, axis=0, keepdims=True)
        gg = r * (gm * gain) - gated * k
        ds_now = gg * (gate * sig)
        grads[:, cols] = (gg * scanned * sig * (1.0 + gate * (1.0 - sig))).astype(bf16)
        dsc[:, cols] = ds_now
        d16[:, cols] = ds_now.astype(bf16)
        skip_parts.append(jnp.sum(ds_now * x, axis=0, keepdims=True))
    gw[:, 1152:] = tn(gb[...], mixed[...]).astype(bf16)
    inner[...] = nt(act[:, 384:512], act[:, 512:640])
    dinner[...] = jnp.zeros(dinner.shape, f32)
    low_lanes = iota((128, 128), 1) < 64
    for jb in range(4):
        i0 = jb * 128
        rows = slice(i0, i0 + 128)
        for p in range(3):
            cols = slice(p * 128, p * 128 + 128)
            outs = []
            xp = xs[rows, cols]
            dp = d16[i0:, cols]
            for h in (2 * p, 2 * p + 1):
                spread = log_t[h : h + 1, i0:] - log_now[rows, h : h + 1] + bias[rows, i0:]
                e = jnp.exp(spread)
                outs.append(nn((inner[rows, i0:] * e).astype(bf16), dp))
                keep = low_lanes if h == 2 * p else jnp.logical_not(low_lanes)
                xh = jnp.where(keep, xp.astype(f32), 0.0).astype(bf16)
                dinner[rows, i0:] = dinner[rows, i0:] + e * nt(xh, dp)
            z[rows, cols] = jnp.where(low_lanes, outs[0], outs[1])
    x32 = act[:, :UNITS].astype(f32)
    zz = z[...]
    dlog = nt(d16[...].astype(f32) * kept_y[...] - xs[...].astype(f32) * zz, spread_heads, highest)
    dstep = nt(x32 * zz, spread_heads, highest)
    da = nn(jnp.where(bias[...] == 0.0, 1.0, 0.0), dlog, highest)
    dstep = dstep + da * rates
    ddt = jnp.where(lane < LOCAL, dstep * jax.nn.sigmoid(step_in), 0.0)
    skip_all = jnp.concatenate(skip_parts, axis=1)
    skip_heads = nt(jnp.broadcast_to(skip_all, (8, UNITS)), spread_heads, highest)
    row = iota((8, 128), 0)
    a_row = jnp.sum(da * steps, axis=0, keepdims=True) * rates
    b_row = jnp.sum(ddt, axis=0, keepdims=True)
    head_out[...] = jnp.where(
        row == 0, a_row, jnp.where(row == 1, b_row, jnp.where(row == 2, skip_heads, 0.0))
    )
    grads[:, 1024:1152] = ddt.astype(bf16)
    din = dinner[...].astype(bf16)
    grad_b = nn(din, act[:, 512:640])
    grad_c = tn(din, act[:, 384:512])
    for c in range(0, CONV, 128):
        cols = slice(c, c + 128)
        if c < UNITS:
            dact = step_wide[:, cols] * z[:, cols] + skip_row[:, cols] * dsc[:, cols]
        else:
            dact = grad_b if c == UNITS else grad_c
        v, y = conv_of(c)
        sig = jax.nn.sigmoid(y)
        dy = dact * sig * (1.0 + y * (1.0 - sig))
        grad_small[4:5, cols] = jnp.sum(dy, axis=0, keepdims=True)
        grad_small[3:4, cols] = jnp.sum(dy * v, axis=0, keepdims=True)
        dv = smalls[3:4, cols] * dy
        for s in (1, 2, 3):
            masked = marks[s - 1] * dy
            grad_small[3 - s : 4 - s, cols] = jnp.sum(
                masked * pltpu.roll(v, s, 0), axis=0, keepdims=True
            )
            dv = dv + smalls[3 - s : 4 - s, cols] * pltpu.roll(masked, TOK - s, 0)
        grads[:, UNITS + c : UNITS + c + 128] = dv.astype(bf16)
    gn[...] = nt(grads[...], weights[:, :1152]).astype(bf16)
    gw[:, :1024] = tn(ng[...], grads[:, :1024]).astype(bf16)
    packed = jnp.zeros((32, 128), f32)
    for tap, width, first, row_at, start in SMALLS:
        values = (
            small_owner(width) * grad_small[row_at : row_at + 1, start : start + width]
        ).astype(bf16)
        packed = packed + nn(values, small_lanes(tap, width, first))
    last = tn(ng[...], grads[:, 1024:1152]) + nn(placing(), packed.astype(bf16))
    gw[:, 1024:1152] = last.astype(bf16)


VM = pl.BlockSpec(memory_space=pltpu.VMEM)


def compute_call(kernel, out_shape, scratch, args, lengths_at):
    specs = [VM] * len(args)
    if lengths_at is not None:
        specs[lengths_at] = pl.BlockSpec(memory_space=pltpu.SMEM)
    return pl.pallas_call(
        kernel,
        out_shape=out_shape,
        in_specs=specs,
        out_specs=[VM] * len(out_shape),
        scratch_shapes=scratch,
        compiler_params=pltpu.CompilerParams(vmem_limit_bytes=28 * 1024 * 1024),
    )(*args)


def shaped(shape, kind=f32):
    return jax.ShapeDtypeStruct(shape, kind)


SHARED = [pltpu.VMEM((3, TOK, 128), f32), pltpu.VMEM((8, 128), f32)]
FORWARD = SHARED + [
    pltpu.VMEM((TOK, TOK), f32),
    pltpu.VMEM((TOK, TOK), f32),
    pltpu.VMEM((TOK, CONV), bf16),
    pltpu.VMEM((TOK, UNITS), bf16),
]
FORWARD_OUT = [
    shaped((TOK, 1152)),
    shaped((TOK, UNITS)),
    shaped((TOK, 128)),
    shaped((8, CONV)),
]
FORWARD_ENDS = [pltpu.VMEM((TOK, D), bf16), pltpu.VMEM((8, TOK), f32)]
BACKWARD = SHARED + [
    pltpu.VMEM((TOK, TOK), f32),
    pltpu.VMEM((TOK, TOK), f32),
    pltpu.VMEM((TOK, TOK), f32),
    pltpu.VMEM((TOK, CONV), bf16),
    pltpu.VMEM((TOK, UNITS), bf16),
    pltpu.VMEM((TOK, UNITS), bf16),
    pltpu.VMEM((TOK, UNITS), bf16),
    pltpu.VMEM((TOK, UNITS), f32),
    pltpu.VMEM((TOK, UNITS), f32),
    pltpu.VMEM((TOK, 1152), bf16),
    pltpu.VMEM((8, CONV), f32),
]
BACKWARD_ENDS = [pltpu.VMEM((TOK, D), bf16), pltpu.VMEM((D, WIDE), bf16), pltpu.VMEM((8, 128), f32)]


class Place:
    def __init__(self):
        self.dp = lax.axis_index("dp")
        self.x = lax.axis_index("tensor")
        self.core = self.dp % 2
        self.other = 1 - self.core
        self.chip = self.dp // 2
        y, z = self.chip % 4, self.chip // 4
        self.a = self.other * y + self.core * z
        self.b = self.other * z + self.core * y
        self.partner = (self.chip * 2 + self.other, self.x)
        self.right = (self.dp, (self.x + 1) % 4)
        self.left = (self.dp, (self.x + 3) % 4)

    def chip_at(self, a, b):
        return self.other * (b * 4 + a) + self.core * (a * 4 + b)

    def partners_chip_at(self, a, b):
        return self.core * (b * 4 + a) + self.other * (a * 4 + b)

    def along_a(self, k):
        return (self.chip_at((self.a + k) % 4, self.b) * 2 + self.core, self.x)

    def along_b(self, k):
        return (self.chip_at(self.a, (self.b + k) % 4) * 2 + self.core, self.x)

    def along_x(self, k):
        return (self.dp, (self.x + k) % 4)


def greet(peers):
    barrier = pltpu.get_barrier_semaphore()
    for peer in peers:
        pl.semaphore_signal(barrier, inc=1, device_id=peer, device_id_type=MESH)


def met_all(peers):
    pl.semaphore_wait(pltpu.get_barrier_semaphore(), len(peers))


def x_peers(at):
    return [at.along_x(k) for k in (1, 2, 3)]


def all_peers(at):
    return (
        [at.partner]
        + [at.along_a(k) for k in (1, 2, 3)]
        + [at.along_b(k) for k in (1, 2, 3)]
        + x_peers(at)
    )


class Sems:
    def __init__(self, send, recv):
        self.send, self.recv, self.used = send, recv, 0

    def copy(self, src, dst, device):
        index = self.used
        self.used += 1
        made = pltpu.make_async_remote_copy(
            src_ref=src,
            dst_ref=dst,
            send_sem=self.send.at[index],
            recv_sem=self.recv.at[index],
            device_id=device,
            device_id_type=MESH,
        )
        made.start()
        return made


def together(order, *parts, ends=True):
    parts = list(parts)
    for index in order:
        next(parts[index], None)
    while ends and parts:
        for part in list(parts):
            try:
                next(part)
            except StopIteration:
                parts.remove(part)


def rows_of(start, count, multiple):
    return pl.ds(pl.multiple_of(start, multiple), count)


def half_rows(block, half):
    return rows_of(block * OWN + half * HALF, HALF, HALF)


def gather_x(at, sems, out):
    def block(b, half):
        return out.at[half_rows(b, half), :]

    x, r, l = at.x, (at.x + 1) % 4, (at.x + 3) % 4
    c0 = sems.copy(block(x, 0), block(x, 0), at.right)
    c1 = sems.copy(block(x, 1), block(x, 1), at.left)
    yield
    c0.wait_send()
    c2 = sems.copy(block(x, 1), block(x, 1), at.right)
    c1.wait_send()
    c3 = sems.copy(block(x, 0), block(x, 0), at.left)
    yield
    c0.wait_recv()
    c4 = sems.copy(block(l, 0), block(l, 0), at.right)
    yield
    c1.wait_recv()
    c5 = sems.copy(block(r, 1), block(r, 1), at.left)
    yield
    for c in (c2, c3, c4, c5):
        c.wait_recv()
    for c in (c2, c3, c4, c5):
        c.wait_send()


def scatter_x(at, sems, up, buf, tmp, total):
    def block(b, half):
        return up.at[half_rows(b, half), :]

    def value(b, half):
        return up[half_rows(b, half), :].astype(f32)

    x, r, l, o = at.x, (at.x + 1) % 4, (at.x + 3) % 4, (at.x + 2) % 4
    c0 = sems.copy(block(o, 0), buf.at[0], at.right)
    c1 = sems.copy(block(o, 1), buf.at[1], at.left)
    yield
    c0.wait_send()
    c2 = sems.copy(block(r, 1), buf.at[2], at.right)
    c1.wait_send()
    c3 = sems.copy(block(l, 0), buf.at[3], at.left)
    yield
    c0.wait_recv()
    tmp[0] = (value(r, 0) + buf[0].astype(f32)).astype(bf16)
    c4 = sems.copy(tmp.at[0], buf.at[4], at.right)
    yield
    c1.wait_recv()
    tmp[1] = (value(l, 1) + buf[1].astype(f32)).astype(bf16)
    c5 = sems.copy(tmp.at[1], buf.at[5], at.left)
    yield
    for c in (c2, c3, c4, c5):
        c.wait_recv()
    total[0:HALF, :] = value(x, 0) + buf[4].astype(f32) + buf[3].astype(f32)
    total[HALF:OWN, :] = value(x, 1) + buf[2].astype(f32) + buf[5].astype(f32)
    for c in (c2, c3, c4, c5):
        c.wait_send()


def share_squares(at, sems, squares, buf):
    def lanes(x):
        return rows_of(x * OWN, OWN, OWN)

    copies = [
        sems.copy(squares.at[:, lanes((at.x + k) % 4)], buf.at[k - 1], at.along_x(k))
        for k in (1, 2, 3)
    ]
    yield
    for c in copies:
        c.wait_recv()
    buf[3] = squares[:, lanes(at.x)] + buf[0] + buf[1] + buf[2]
    for c in copies:
        c.wait_send()


def share_rows(at, sems, rk):
    copies = [sems.copy(rk.at[at.x], rk.at[at.x], at.along_x(k)) for k in (1, 2, 3)]
    yield
    for c in copies:
        c.wait_recv()
    for c in copies:
        c.wait_send()


def gather_weights(at, sems, shard, met, out):
    mine = rows_of(at.core * HALFW, HALFW, HALFW)

    def block(chip):
        return out.at[rows_of(chip * PAIR, PAIR, PAIR), mine]

    first = sems.copy(shard, met, at.partner)
    yield
    first.wait_recv()
    core = at.core.astype(f32)
    own, theirs = shard[0:ROWS, :].astype(f32), met[0:ROWS, :].astype(f32)
    low = own * (1.0 - core) + theirs * core
    high = own * core + theirs * (1.0 - core)
    out[rows_of(at.chip * PAIR, PAIR, PAIR), :] = jnp.concatenate([low, high], axis=0).astype(bf16)
    along_a = [None] + [sems.copy(block(at.chip), block(at.chip), at.along_a(k)) for k in (1, 2, 3)]
    along_b = []
    passed = []
    for k in range(4):
        if k:
            yield
            along_a[k].wait_recv()
        now = block(at.chip_at((at.a + 4 - k) % 4, at.b))
        for j in (1, 2, 3):
            along_b.append((k, j, sems.copy(now, now, at.along_b(j))))
        if k:
            passed.append(sems.copy(now, now, at.partner))
    for k, j, c in along_b:
        yield
        c.wait_recv()
        now = block(at.chip_at((at.a + 4 - k) % 4, (at.b + 4 - j) % 4))
        passed.append(sems.copy(now, now, at.partner))
    yield
    for c in passed:
        c.wait_recv()
    for c in [first] + along_a[1:] + [c for _, _, c in along_b] + passed:
        c.wait_send()


def scatter_weights(at, sems, grads, out, met, held, got, sums, got_last, final, met_final, xsend, xgot):
    mine = rows_of(at.core * HALFW, HALFW, HALFW)
    others = rows_of(at.other * HALFW, HALFW, HALFW)

    def rows(chip):
        return rows_of(chip * PAIR, PAIR, PAIR)

    order = [(j, m) for j in (1, 2, 3, 0) for m in range(4)]
    first = []
    for j, m in order:
        chip = at.partners_chip_at(m, (at.a + j) % 4)
        first.append(sems.copy(grads.at[rows(chip), others], met.at[rows(chip), :], at.partner))
    second = []
    yield
    for (j, m), c in zip(order, first):
        c.wait_recv()
        chip = at.chip_at(m, (at.b + j) % 4)
        both = grads[rows(chip), mine].astype(f32) + met[rows(chip), :].astype(f32)
        held[j, m] = both.astype(bf16)
        if j:
            second.append(sems.copy(held.at[j, m], got.at[j - 1, m], at.along_b(j)))
    yield
    for c in second:
        c.wait_recv()

    def summed(m):
        return (
            held[0, m].astype(f32)
            + got[0, m].astype(f32)
            + got[1, m].astype(f32)
            + got[2, m].astype(f32)
        )

    third = []
    for k in (1, 2, 3):
        sums[k] = summed((at.a + k) % 4).astype(bf16)
        third.append(sems.copy(sums.at[k], got_last.at[k - 1], at.along_a(k)))
    last = summed(at.a)
    yield
    for c in third:
        c.wait_recv()
    final[...] = (
        last
        + got_last[0].astype(f32)
        + got_last[1].astype(f32)
        + got_last[2].astype(f32)
    )
    fourth = sems.copy(final.at[rows_of(at.other * ROWS, ROWS, 8), :], met_final, at.partner)
    out[:, mine] = final[rows_of(at.core * ROWS, ROWS, 8), :]
    yield
    fourth.wait_recv()
    out[:, others] = met_final[...]
    xsend[...] = out[:, 768:1152]
    fifth = [sems.copy(xsend, xgot.at[k - 1], at.along_x(k)) for k in (1, 2, 3)]
    yield
    for c in fifth:
        c.wait_recv()
    lane = iota((ROWS, 384), 1)
    shared = (lane < 256) | ((lane >= 256 + 66) & (lane < 256 + 106))
    out[:, 768:1152] = xsend[...] + jnp.where(shared, xgot[0] + xgot[1] + xgot[2], 0.0)
    for c in first + second + third + [fourth] + fifth:
        c.wait_send()


def sum_everywhere(at, sems, values, held, got):
    held[0] = values[...]
    slot = 0
    stages = [
        [at.partner],
        [at.along_a(k) for k in (1, 2, 3)],
        [at.along_b(k) for k in (1, 2, 3)],
        [at.along_x(k) for k in (1, 2, 3)],
    ]
    for stage, peers in enumerate(stages):
        copies = []
        for peer in peers:
            copies.append(sems.copy(held.at[stage], got.at[slot], peer))
            slot += 1
        yield
        for c in copies:
            c.wait_recv()
        more = got[slot - len(peers)]
        for s in range(slot - len(peers) + 1, slot):
            more = more + got[s]
        if stage == 3:
            more = jnp.where(iota((32, 128), 0) < 16, more, 0.0)
        held[stage + 1] = held[stage] + more
        for c in copies:
            c.wait_send()
    values[...] = held[4]


def row_scale(values):
    return lax.rsqrt(jnp.mean(values * values, axis=-1, keepdims=True) + epsilon)


def put_own(at, out, values):
    out[rows_of(at.x * OWN, OWN, OWN), :] = values


def put_rows(at, rk, r, k):
    row = iota((8, 128), 0)
    rk[at.x] = jnp.where(row == 0, to_row(r), jnp.where(row == 1, to_row(k), 0.0))


def pack_shard(layer, w_zx, w_bc, w_dt, conv_x, conv_bc, gate_gain, w_out, spare, shard):
    spare[...] = jnp.zeros(spare.shape, f32)
    spare[0:LOCAL, 0:ROWS] = w_dt[:, layer, :].astype(f32)
    spare[...] = spare[...].T
    at = LOCAL
    for tap in range(5):
        values = conv_x[layer, tap].astype(f32)
        for e in range(2):
            spare[0:1, at : at + LOCAL] = values[e : e + 1, :]
            at += LOCAL
    for tap in range(5):
        spare[0:1, at : at + 8] = conv_bc[tap].astype(f32)[layer : layer + 1, :]
        at += 8
    values = gate_gain[layer].astype(f32)
    for e in range(2):
        spare[0:1, at : at + LOCAL] = values[e : e + 1, :]
        at += LOCAL
    gates, signals = w_zx[layer, :, 0, :].astype(f32), w_zx[layer, :, 1, :].astype(f32)
    sides = [gates, signals, w_bc[layer].astype(f32), spare[0:ROWS, :], w_out[layer].astype(f32)]
    whole = jnp.concatenate(sides, axis=1)
    below = jnp.zeros((32 - ROWS, WIDE), f32)
    shard[...] = jnp.concatenate([whole, below], axis=0).astype(bf16)


def start_kernel(
    tokens, gains, cot, w_zx, w_bc, w_dt, conv_x, conv_bc, gate_gain, w_out,
    weights, ng, gb, shard1,
    shard, spare, met, send, recv,
):
    at = Place()
    sems = Sems(send, recv)
    parts = (w_zx, w_bc, w_dt, conv_x, conv_bc, gate_gain, w_out, spare)
    greet(all_peers(at))
    pack_shard(0, *parts, shard)
    met_all(all_peers(at))
    moving = gather_weights(at, sems, shard, met, weights)
    next(moving)
    stream = tokens[...].astype(f32)
    put_own(at, ng, (stream * row_scale(stream) * gains[0:1, :]).astype(bf16))
    put_own(at, gb, cot[...])
    first, second = gather_x(at, sems, ng), gather_x(at, sems, gb)
    def packing():
        pack_shard(1, *parts, shard1)
        yield

    together([1, 0, 1, 2, 0, 0, 0, 2, 1, 1, 3, 2, 2], moving, first, second, packing())


def gate_scale(sqbuf):
    return to_column(lax.rsqrt(sqbuf[3][0:1, :] / DI + epsilon))


def middle_kernel(*refs):
    ins, tokens, gains, shard = refs[:6], *refs[6:9]
    kept, (stream1, branch0, r0, ng, weights) = refs[9:13], refs[13:18]
    work, (up, squares) = refs[18:24], refs[24:26]
    met, buf, tmp, total, sqbuf, send, recv = refs[26:]
    at = Place()
    sems = Sems(send, recv)
    greet(all_peers(at))
    here = forward_steps(0, *ins, *kept, up, squares, *work)
    next(here)
    met_all(all_peers(at))
    moving = gather_weights(at, sems, shard, met, weights)
    together([1, 0, 0, 1, 0, 0, 0, 0, 0, 0], here, moving, ends=False)

    def along():
        yield from scatter_x(at, sems, up, buf, tmp, total)
        r = gate_scale(sqbuf)
        branch = r * total[...]
        stream = tokens[...].astype(f32) + branch
        branch0[...] = branch
        stream1[...] = stream
        r0[...] = jnp.broadcast_to(to_row(r), (8, 128))
        put_own(at, ng, (stream * row_scale(stream) * gains[1:2, :]).astype(bf16))
        yield from gather_x(at, sems, ng)

    together(
        [0, 1, 2, 2, 2, 1, 1, 1, 0, 1, 1, 1, 1],
        share_squares(at, sems, squares, sqbuf),
        along(),
        moving,
    )


def turn_kernel(*refs):
    ins, stream1, cot = refs[:6], *refs[6:8]
    kept, (block_out, rk) = refs[8:12], refs[12:14]
    work, (up, squares) = refs[14:20], refs[20:22]
    buf, tmp, total, sqbuf, send, recv = refs[22:]
    at = Place()
    sems = Sems(send, recv)
    greet(x_peers(at))
    together([], forward_steps(1, *ins, *kept, up, squares, *work))
    met_all(x_peers(at))
    together(
        [0, 1, 1, 1, 1, 0],
        share_squares(at, sems, squares, sqbuf),
        scatter_x(at, sems, up, buf, tmp, total),
    )
    r = gate_scale(sqbuf)
    branch = r * total[...]
    block_out[...] = (stream1[...] + branch).astype(bf16)
    dots = jnp.sum(cot[...].astype(f32) * branch, axis=1, keepdims=True)
    put_rows(at, rk, r, r * r * dots / DI)
    together([], share_rows(at, sems, rk))


def norm_back(gnorm, stream, gain, grad):
    q = row_scale(stream)
    gain_row = jnp.sum(gnorm * stream * q, axis=0, keepdims=True)
    rows = gnorm * gain
    inner = jnp.mean(rows * stream, axis=1, keepdims=True)
    return grad + q * rows - stream * (q * q * q) * inner, gain_row


def back_kernel(*refs):
    ins, stream1, gains, cot, branch0, r0 = refs[:12], *refs[12:17]
    (grad0, gb, rk, gg, out, head), work = refs[17:23], refs[23:36]
    (gn, gw), (buf, tmp, total), rest = refs[36:38], refs[38:41], refs[41:]
    at = Place()
    sems = Sems(*rest[-2:])
    greet(all_peers(at))
    backward_steps(1, *ins, gn, gw, head, *work)
    met_all(all_peers(at))

    def along():
        yield from scatter_x(at, sems, gn, buf, tmp, total)
        grad, gain_row = norm_back(
            total[...], stream1[...], gains[1:2, :], cot[...].astype(f32)
        )
        low = grad.astype(bf16)
        put_own(at, gb, low)
        sharing = gather_x(at, sems, gb)
        next(sharing)
        grad0[...] = grad
        r = to_column(r0[0:1, :])
        dots = jnp.sum(low.astype(f32) * branch0[...], axis=1, keepdims=True)
        put_rows(at, rk, r, r * r * dots / DI)
        rows = share_rows(at, sems, rk)
        next(rows)
        gg[...] = jnp.zeros(gg.shape, f32)
        for c in range(6):
            gg[c : c + 1, :] = gain_row[:, c * 128 : c * 128 + 128]
        yield
        yield from sharing
        yield from rows

    together(
        [0, 1, 0, 1, 0, 0, 0, 0, 1, 1, 0, 0, 1],
        along(),
        scatter_weights(at, sems, gw, out, *rest[:-2]),
    )


def end_kernel(*refs):
    ins, tokens, gains, grad0, gg1, head1 = refs[:12], *refs[12:17]
    (input_grad, out, values), work = refs[17:20], refs[20:33]
    (gn, gw, head0), (buf, tmp, total, held, got), rest = refs[33:36], refs[36:41], refs[41:]
    at = Place()
    sems = Sems(*rest[-2:])
    greet(all_peers(at))
    backward_steps(0, *ins, gn, gw, head0, *work)
    met_all(all_peers(at))

    def along():
        yield from scatter_x(at, sems, gn, buf, tmp, total)
        grad, gain_row = norm_back(
            total[...], tokens[...].astype(f32), gains[0:1, :], grad0[...]
        )
        input_grad[...] = grad
        values[...] = jnp.zeros(values.shape, f32)
        for c in range(6):
            values[c : c + 1, :] = gain_row[:, c * 128 : c * 128 + 128]
        values[6:12, :] = gg1[0:6, :]
        values[16:24, :] = head0[...]
        values[24:32, :] = head1[...]
        yield from sum_everywhere(at, sems, values, held, got)

    together(
        [0, 1, 0, 1, 0, 0, 0, 1, 0, 1, 0, 1, 0],
        along(),
        scatter_weights(at, sems, gw, out, *rest[:-2]),
    )


def send_call(kernel, number, copies, out_shape, scratch, args, lengths_at=None):
    specs = [VM] * len(args)
    if lengths_at is not None:
        specs[lengths_at] = pl.BlockSpec(memory_space=pltpu.SMEM)
    return pl.pallas_call(
        kernel,
        out_shape=out_shape,
        in_specs=specs,
        out_specs=[VM] * len(out_shape),
        scratch_shapes=scratch
        + [pltpu.SemaphoreType.DMA((copies,)), pltpu.SemaphoreType.DMA((copies,))],
        compiler_params=pltpu.CompilerParams(
            collective_id=number, has_side_effects=True, vmem_limit_bytes=28 * 1024 * 1024
        ),
    )(*args)


RING = [
    pltpu.VMEM((6, HALF, D), bf16),
    pltpu.VMEM((2, HALF, D), bf16),
    pltpu.VMEM((OWN, D), f32),
]
SCATTER = [
    pltpu.VMEM((D, HALFW), bf16),
    pltpu.VMEM((4, 4, PAIR, HALFW), bf16),
    pltpu.VMEM((3, 4, PAIR, HALFW), bf16),
    pltpu.VMEM((4, PAIR, HALFW), bf16),
    pltpu.VMEM((3, PAIR, HALFW), bf16),
    pltpu.VMEM((PAIR, HALFW), f32),
    pltpu.VMEM((ROWS, HALFW), f32),
    pltpu.VMEM((ROWS, 384), f32),
    pltpu.VMEM((3, ROWS, 384), f32),
]


def finish_kernel(
    sum0, sum1, values, block_in, grad_in,
    block_out, input_grad, norm_gain, zx, bc, dt, conv_x, conv_bc, a_log, dt_bias, d_skip, gate_gain, w_out,
):
    block_out[...] = block_in[...]
    input_grad[...] = grad_in[...]
    for layer, total in enumerate((sum0, sum1)):
        for c in range(6):
            norm_gain[layer : layer + 1, c * 128 : c * 128 + 128] = values[
                layer * 6 + c : layer * 6 + c + 1, :
            ]
        row = 16 + 8 * layer
        for k, out in enumerate((a_log, dt_bias, d_skip)):
            out[layer : layer + 1, :] = values[row + k : row + k + 1, 0:LOCAL]
        zx[layer, :, 0, :] = total[:, 0:UNITS]
        zx[layer, :, 1, :] = total[:, UNITS:768]
        bc[layer] = total[:, 768:1024]
        w_out[layer] = total[:, 1152:]
        spread = total[:, 1024:1152]
        wide = jnp.concatenate([spread, jnp.zeros((128 - ROWS, 128), f32)], axis=0).T
        dt[:, layer, :] = wide[0:LOCAL, 0:ROWS]
        small = total[0:1, 1024:1152]
        at = LOCAL
        for tap in range(5):
            for e in range(2):
                conv_x[layer, tap, e : e + 1, :] = small[:, at : at + LOCAL]
                at += LOCAL
        for tap in range(5):
            conv_bc[tap, layer : layer + 1, :] = small[:, at : at + 8]
            at += 8
        for e in range(2):
            gate_gain[layer, e : e + 1, :] = small[:, at : at + LOCAL]
            at += LOCAL


def body(
    tokens,
    lengths,
    norm_gain,
    w_zx,
    w_bc,
    w_dt,
    conv_x,
    conv_bc,
    a_log,
    dt_bias,
    d_skip,
    gate_gain,
    w_out,
    cotangent,
):
    small = (lengths, dt_bias, a_log, d_skip)
    weights0, ng0, gb1, shard1 = send_call(
        start_kernel,
        0,
        43,
        [
            shaped((D, WIDE), bf16),
            shaped((TOK, D), bf16),
            shaped((TOK, D), bf16),
            shaped((32, WIDE), bf16),
        ],
        [
            pltpu.VMEM((32, WIDE), bf16),
            pltpu.VMEM((128, 128), f32),
            pltpu.VMEM((32, WIDE), bf16),
        ],
        (
            tokens,
            norm_gain,
            cotangent,
            w_zx,
            w_bc,
            w_dt.transpose(2, 0, 1),
            conv_x.swapaxes(2, 3),
            conv_bc.swapaxes(0, 1),
            gate_gain.swapaxes(1, 2),
            w_out.swapaxes(1, 2),
        ),
    )
    *kept0, stream1, branch0, r0, ng1, weights1 = send_call(
        middle_kernel,
        1,
        46,
        FORWARD_OUT
        + [
            shaped((OWN, D)),
            shaped((OWN, D)),
            shaped((8, 128)),
            shaped((TOK, D), bf16),
            shaped((D, WIDE), bf16),
        ],
        FORWARD
        + FORWARD_ENDS
        + [pltpu.VMEM((32, WIDE), bf16)]
        + RING
        + [pltpu.VMEM((4, 8, 128), f32)],
        (ng0, weights0, *small, tokens, norm_gain, shard1),
        2,
    )
    *kept1, block_out, rk1 = send_call(
        turn_kernel,
        2,
        12,
        FORWARD_OUT + [shaped((OWN, D), bf16), shaped((4, 8, 128))],
        FORWARD + FORWARD_ENDS + RING + [pltpu.VMEM((4, 8, 128), f32)],
        (ng1, weights1, *small, stream1, cotangent),
        2,
    )
    grad0, gb0, rk0, gg1, sum1, head1 = send_call(
        back_kernel,
        3,
        50,
        [
            shaped((OWN, D)),
            shaped((TOK, D), bf16),
            shaped((4, 8, 128)),
            shaped((8, 128)),
            shaped((ROWS, WIDE)),
            shaped((8, 128)),
        ],
        BACKWARD + BACKWARD_ENDS[:2] + RING + SCATTER,
        (gb1, ng1, weights1, *small, *kept1, rk1, stream1, norm_gain, cotangent, branch0, r0),
        3,
    )
    input_grad, sum0, values = send_call(
        end_kernel,
        4,
        51,
        [shaped((OWN, D)), shaped((ROWS, WIDE)), shaped((32, 128))],
        BACKWARD
        + BACKWARD_ENDS
        + RING
        + [pltpu.VMEM((5, 32, 128), f32), pltpu.VMEM((10, 32, 128), f32)]
        + SCATTER,
        (gb0, ng0, weights0, *small, *kept0, rk0, tokens, norm_gain, grad0, gg1, head1),
        3,
    )
    outs = compute_call(
        finish_kernel,
        [
            shaped((OWN, D), bf16),
            shaped((OWN, D)),
            shaped((2, D)),
            shaped((2, ROWS, 2, UNITS)),
            shaped((2, ROWS, 256)),
            shaped((LOCAL, 2, ROWS)),
            shaped((2, 5, 2, LOCAL)),
            shaped((5, 2, 8)),
            shaped((2, LOCAL)),
            shaped((2, LOCAL)),
            shaped((2, LOCAL)),
            shaped((2, 2, LOCAL)),
            shaped((2, ROWS, UNITS)),
        ],
        [],
        (sum0, sum1, values, block_out, input_grad),
        None,
    )
    block_out, input_grad, g_norm, g_zx, g_bc, g_dt, g_cx, g_cb, g_a, g_b, g_d, g_gate, g_out = outs
    return (
        block_out,
        input_grad,
        g_norm,
        g_zx,
        g_bc,
        g_dt.transpose(1, 2, 0),
        g_cx.swapaxes(2, 3),
        g_cb.swapaxes(0, 1),
        g_a,
        g_b,
        g_d,
        g_gate.swapaxes(1, 2),
        g_out.swapaxes(1, 2),
    )


def solution(mesh):
    return jax.shard_map(
        body,
        mesh=mesh,
        in_specs=(
            P(("dp", "tensor"), None),
            P("dp", None),
            P(),
            P(None, "dp", None, "tensor"),
            P(None, "dp", None),
            P(None, "dp", "tensor"),
            P(None, None, "tensor", "dp"),
            P(None, None, "dp"),
            P(None, "tensor"),
            P(None, "tensor"),
            P(None, "tensor"),
            P(None, "tensor", "dp"),
            P(None, "tensor", "dp"),
            P(("dp", "tensor"), None),
        ),
        out_specs=(
            P(("dp", "tensor"), None),
            P(("dp", "tensor"), None),
            P(),
            P(None, "dp", None, "tensor"),
            P(None, "dp", None),
            P(None, "dp", "tensor"),
            P(None, None, "tensor", "dp"),
            P(None, None, "dp"),
            P(None, "tensor"),
            P(None, "tensor"),
            P(None, "tensor"),
            P(None, "tensor", "dp"),
            P(None, "tensor", "dp"),
        ),
        check_vma=False,
    )
```

```python
import functools
from types import SimpleNamespace

import jax
import jax.numpy as jnp
from jax import lax
from jax.experimental import pallas as pl
from jax.experimental.pallas import tpu as pltpu
from jax.sharding import PartitionSpec as P

D = 768
HEADS = 24
DI = 1536
LOCAL = 6
UNITS = 384
CONV = 640
TOK = 512
OWN = 128
HALF = 64
ROWS = 24
PAIR = 48
WIDE = 1536
HALFW = 768
MESH = pl.DeviceIdType.MESH
epsilon = 1e-05
highest = lax.Precision.HIGHEST
f32 = jnp.float32
bf16 = jnp.bfloat16
FAR = -1e30
LIMIT = 62 * 1024 * 1024
VM = pl.BlockSpec(memory_space=pltpu.VMEM)


def nn(a, b, precision=None):
    return lax.dot_general(
        a, b, (((1,), (0,)), ((), ())), precision=precision, preferred_element_type=f32
    )


def nt(a, b, precision=None):
    return lax.dot_general(
        a, b, (((1,), (1,)), ((), ())), precision=precision, preferred_element_type=f32
    )


def tn(a, b, precision=None):
    return lax.dot_general(
        a, b, (((0,), (0,)), ((), ())), precision=precision, preferred_element_type=f32
    )


def iota(shape, dim):
    return lax.broadcasted_iota(jnp.int32, shape, dim)


def softplus(v):
    return jnp.maximum(v, 0.0) + jnp.log1p(jnp.exp(-jnp.abs(v)))


def one_hot(condition, kind=f32):
    return jnp.where(condition, 1.0, 0.0).astype(kind)


def head_spread():
    return one_hot((iota((128, UNITS), 1) >> 6) == iota((128, UNITS), 0))


def to_row(column):
    eye = iota((128, 128), 0) == iota((128, 128), 1)
    return jnp.sum(jnp.where(eye, column, 0.0), axis=0, keepdims=True)


def to_column(row):
    eye = iota((128, 128), 0) == iota((128, 128), 1)
    return jnp.sum(jnp.where(eye, row, 0.0), axis=1, keepdims=True)


def small_lanes(tap, width, first):
    unit = iota((width, 128), 0)
    lane = iota((width, 128), 1)
    if width == UNITS:
        place = 6 + first + tap * 12 + (unit & 1) * 6 + (unit >> 6)
    else:
        place = 6 + first + tap * 8 + (unit & 7)
    return one_hot(lane == place, bf16)


def small_owner(width):
    unit = iota((32, width), 1)
    owner = (unit & 63) >> 1 if width == UNITS else unit >> 3
    return one_hot(owner == iota((32, width), 0))


SMALLS = (
    [(tap, UNITS, 0, tap, 0) for tap in range(5)]
    + [(tap, 256, 60, tap, UNITS) for tap in range(5)]
    + [(0, UNITS, 100, 5, 0)]
)


def placing():
    return one_hot(iota((D, 32), 0) == iota((D, 32), 1) * ROWS, bf16)


def segment_starts(lengths, position):
    first = lengths[0, 0]
    second = first + lengths[0, 1]
    return jnp.where(position >= second, second, jnp.where(position >= first, first, 0))


def fill_masks(lengths, marks, bias, bias_t):
    position = iota((TOK, 128), 0)
    since = position - segment_starts(lengths, position)
    for s in (1, 2, 3):
        marks[s - 1] = one_hot(since >= s)
    for b in range(4):
        rows = slice(b * 128, b * 128 + 128)
        here, there = iota((128, TOK), 0) + b * 128, iota((128, TOK), 1)
        linked = (there <= here) & (there >= segment_starts(lengths, here))
        bias[rows, :] = jnp.where(linked, 0.0, FAR)
        linked = (here <= there) & (here >= segment_starts(lengths, there))
        bias_t[rows, :] = jnp.where(linked, 0.0, FAR)


def forward_steps(
    layer, ng, weights, heads_all,
    proj, kept_y, logs, smalls, up, squares,
    marks, bias, inner, act, xs,
):
    heads = heads_all.at[layer]
    proj[...] = nn(ng[...], weights[:, :1152])
    yield
    packed = tn(placing(), weights[:, 1024:1152]).astype(bf16)
    smalls[...] = jnp.zeros(smalls.shape, f32)
    for tap, width, first, row, start in SMALLS:
        spread = nt(packed, small_lanes(tap, width, first)) * small_owner(width)
        smalls[row : row + 1, start : start + width] = jnp.sum(spread, axis=0, keepdims=True)
    yield
    lane = iota((TOK, 128), 1)
    steps = jnp.where(lane < LOCAL, softplus(proj[:, 1024:1152] + heads[0:1, :]), 0.0)
    rates = jnp.where(iota((1, 128), 1) < LOCAL, -jnp.exp(heads[1:2, :]), 0.0)
    log_now = nn(jnp.where(bias[...] == 0.0, 1.0, 0.0), steps * rates, highest)
    logs[...] = log_now
    log_t = log_now.T
    for c in range(0, CONV, 128):
        cols = slice(c, c + 128)
        v = proj[:, UNITS + c : UNITS + c + 128]
        y = smalls[4:5, cols] + smalls[3:4, cols] * v
        for s in (1, 2, 3):
            y = y + smalls[3 - s : 4 - s, cols] * (marks[s - 1] * pltpu.roll(v, s, 0))
        act[:, cols] = (y * jax.nn.sigmoid(y)).astype(bf16)
    yield
    spread_heads = head_spread()
    skip_row = nn(heads[...], spread_heads, highest)[2:3, :]
    xs[...] = (act[:, :UNITS].astype(f32) * nn(steps, spread_heads, highest)).astype(bf16)
    inner[...] = nt(act[:, 512:640], act[:, 384:512])
    yield
    for ib in range(4):
        rows = slice(ib * 128, ib * 128 + 128)
        n = ib * 128 + 128
        for p in range(3):
            outs = []
            for h in (2 * p, 2 * p + 1):
                spread = log_now[rows, h : h + 1] - log_t[h : h + 1, :n] + bias[rows, :n]
                g = (inner[rows, :n] * jnp.exp(spread)).astype(bf16)
                outs.append(nn(g, xs[:n, p * 128 : p * 128 + 128]))
            kept_y[rows, p * 128 : p * 128 + 128] = jnp.where(
                iota((128, 128), 1) < 64, outs[0], outs[1]
            )
        yield
    total = jnp.zeros((8, TOK), f32)
    for p in range(3):
        cols = slice(p * 128, p * 128 + 128)
        gate = proj[:, cols]
        scanned = kept_y[:, cols] + skip_row[:, cols] * act[:, cols].astype(f32)
        gated = scanned * (gate * jax.nn.sigmoid(gate))
        total = total + nt(jnp.ones((8, 128), f32), gated * gated, highest)
        xs[:, cols] = (gated * smalls[5:6, cols]).astype(bf16)
    squares[...] = total
    up[...] = nt(xs[...], weights[:, 1152:]).astype(bf16)


def backward_steps(
    layer,
    gb,
    ng,
    weights,
    heads_all,
    proj,
    kept_y,
    logs,
    smalls,
    rk,
    gn,
    gw,
    head_out,
    marks,
    bias,
    inner,
    dinner,
    act,
    xs,
    d16,
    mixed,
    z,
    dsc,
    grads,
    grad_small,
):
    heads = heads_all.at[layer]
    lane = iota((TOK, 128), 1)
    step_in = proj[:, 1024:1152] + heads[0:1, :]
    steps = jnp.where(lane < LOCAL, softplus(step_in), 0.0)
    rates = jnp.where(iota((1, 128), 1) < LOCAL, -jnp.exp(heads[1:2, :]), 0.0)
    log_now = logs[...]
    log_t = log_now.T
    spread_heads = head_spread()
    skip_row = nn(heads[...], spread_heads, highest)[2:3, :]
    step_wide = nn(steps, spread_heads, highest)

    def conv_of(c):
        cols = slice(c, c + 128)
        v = proj[:, UNITS + c : UNITS + c + 128]
        y = smalls[4:5, cols] + smalls[3:4, cols] * v
        for s in (1, 2, 3):
            y = y + smalls[3 - s : 4 - s, cols] * (marks[s - 1] * pltpu.roll(v, s, 0))
        return v, y

    for c in range(0, CONV, 128):
        v, y = conv_of(c)
        act[:, c : c + 128] = (y * jax.nn.sigmoid(y)).astype(bf16)
    xs[...] = (act[:, :UNITS].astype(f32) * step_wide).astype(bf16)
    yield
    z[...] = nn(gb[...], weights[:, 1152:])
    yield
    r = jnp.concatenate([to_column(rk[b, 0:1, :]) for b in range(4)], axis=0)
    k = jnp.concatenate([to_column(rk[b, 1:2, :]) for b in range(4)], axis=0)
    head_rows = jnp.zeros((8, 128), f32)
    grad_small[...] = jnp.zeros(grad_small.shape, f32)
    skip_parts = []
    for p in range(3):
        cols = slice(p * 128, p * 128 + 128)
        gate = proj[:, cols]
        sig = jax.nn.sigmoid(gate)
        x = act[:, cols].astype(f32)
        scanned = kept_y[:, cols] + skip_row[:, cols] * x
        gated = scanned * (gate * sig)
        gain = smalls[5:6, cols]
        gm = z[:, cols]
        scaled = gated * r
        mixed[:, cols] = (scaled * gain).astype(bf16)
        grad_small[5:6, cols] = jnp.sum(gm * scaled, axis=0, keepdims=True)
        gg = r * (gm * gain) - gated * k
        ds_now = gg * (gate * sig)
        grads[:, cols] = (gg * scanned * sig * (1.0 + gate * (1.0 - sig))).astype(bf16)
        dsc[:, cols] = ds_now
        d16[:, cols] = ds_now.astype(bf16)
        skip_parts.append(jnp.sum(ds_now * x, axis=0, keepdims=True))
    yield
    gw[:, 1152:] = tn(gb[...], mixed[...]).astype(bf16)
    yield
    inner[...] = nt(act[:, 384:512], act[:, 512:640])
    dinner[...] = jnp.zeros(dinner.shape, f32)
    low_lanes = iota((128, 128), 1) < 64
    for jb in range(4):
        i0 = jb * 128
        rows = slice(i0, i0 + 128)
        for p in range(3):
            cols = slice(p * 128, p * 128 + 128)
            outs = []
            xp = xs[rows, cols]
            dp = d16[i0:, cols]
            for h in (2 * p, 2 * p + 1):
                spread = log_t[h : h + 1, i0:] - log_now[rows, h : h + 1] + bias[rows, i0:]
                e = jnp.exp(spread)
                outs.append(nn((inner[rows, i0:] * e).astype(bf16), dp))
                keep = low_lanes if h == 2 * p else jnp.logical_not(low_lanes)
                xh = jnp.where(keep, xp.astype(f32), 0.0).astype(bf16)
                dinner[rows, i0:] = dinner[rows, i0:] + e * nt(xh, dp)
            z[rows, cols] = jnp.where(low_lanes, outs[0], outs[1])
        yield
    x32 = act[:, :UNITS].astype(f32)
    zz = z[...]
    dlog = nt(d16[...].astype(f32) * kept_y[...] - xs[...].astype(f32) * zz, spread_heads, highest)
    dstep = nt(x32 * zz, spread_heads, highest)
    da = nn(jnp.where(bias[...] == 0.0, 1.0, 0.0), dlog, highest)
    dstep = dstep + da * rates
    ddt = jnp.where(lane < LOCAL, dstep * jax.nn.sigmoid(step_in), 0.0)
    skip_all = jnp.concatenate(skip_parts, axis=1)
    skip_heads = nt(jnp.broadcast_to(skip_all, (8, UNITS)), spread_heads, highest)
    row = iota((8, 128), 0)
    a_row = jnp.sum(da * steps, axis=0, keepdims=True) * rates
    b_row = jnp.sum(ddt, axis=0, keepdims=True)
    head_out[...] = jnp.where(
        row == 0, a_row, jnp.where(row == 1, b_row, jnp.where(row == 2, skip_heads, 0.0))
    )
    grads[:, 1024:1152] = ddt.astype(bf16)
    yield
    din = dinner[...].astype(bf16)
    grad_b = nn(din, act[:, 512:640])
    grad_c = tn(din, act[:, 384:512])
    for c in range(0, CONV, 128):
        cols = slice(c, c + 128)
        if c < UNITS:
            dact = step_wide[:, cols] * z[:, cols] + skip_row[:, cols] * dsc[:, cols]
        else:
            dact = grad_b if c == UNITS else grad_c
        v, y = conv_of(c)
        sig = jax.nn.sigmoid(y)
        dy = dact * sig * (1.0 + y * (1.0 - sig))
        grad_small[4:5, cols] = jnp.sum(dy, axis=0, keepdims=True)
        grad_small[3:4, cols] = jnp.sum(dy * v, axis=0, keepdims=True)
        dv = smalls[3:4, cols] * dy
        for s in (1, 2, 3):
            masked = marks[s - 1] * dy
            grad_small[3 - s : 4 - s, cols] = jnp.sum(
                masked * pltpu.roll(v, s, 0), axis=0, keepdims=True
            )
            dv = dv + smalls[3 - s : 4 - s, cols] * pltpu.roll(masked, TOK - s, 0)
        grads[:, UNITS + c : UNITS + c + 128] = dv.astype(bf16)
    yield
    gn[...] = nt(grads[...], weights[:, :1152]).astype(bf16)
    yield
    gw[:, :1024] = tn(ng[...], grads[:, :1024]).astype(bf16)
    packed = jnp.zeros((32, 128), f32)
    for tap, width, first, row_at, start in SMALLS:
        values = (
            small_owner(width) * grad_small[row_at : row_at + 1, start : start + width]
        ).astype(bf16)
        packed = packed + nn(values, small_lanes(tap, width, first))
    last = tn(ng[...], grads[:, 1024:1152]) + nn(placing(), packed.astype(bf16))
    gw[:, 1024:1152] = last.astype(bf16)


VM = pl.BlockSpec(memory_space=pltpu.VMEM)


def shaped(shape, kind=f32):
    return jax.ShapeDtypeStruct(shape, kind)


class Place:
    def __init__(self):
        self.dp = lax.axis_index("dp")
        self.x = lax.axis_index("tensor")
        self.core = self.dp % 2
        self.other = 1 - self.core
        self.chip = self.dp // 2
        y, z = self.chip % 4, self.chip // 4
        self.a = self.other * y + self.core * z
        self.b = self.other * z + self.core * y
        self.partner = (self.chip * 2 + self.other, self.x)
        self.right = (self.dp, (self.x + 1) % 4)
        self.left = (self.dp, (self.x + 3) % 4)

    def chip_at(self, a, b):
        return self.other * (b * 4 + a) + self.core * (a * 4 + b)

    def partners_chip_at(self, a, b):
        return self.core * (b * 4 + a) + self.other * (a * 4 + b)

    def along_a(self, k):
        return (self.chip_at((self.a + k) % 4, self.b) * 2 + self.core, self.x)

    def along_b(self, k):
        return (self.chip_at(self.a, (self.b + k) % 4) * 2 + self.core, self.x)

    def across(self, k):
        return (self.chip * 2 + self.other, (self.x + k) % 4)

    def along_x(self, k):
        return (self.dp, (self.x + k) % 4)


def greet(peers):
    barrier = pltpu.get_barrier_semaphore()
    for peer in peers:
        pl.semaphore_signal(barrier, inc=1, device_id=peer, device_id_type=MESH)


def met_all(peers):
    pl.semaphore_wait(pltpu.get_barrier_semaphore(), len(peers))


def x_peers(at):
    return [at.along_x(k) for k in (1, 2, 3)]


def all_peers(at):
    return (
        [at.partner]
        + [at.along_a(k) for k in (1, 2, 3)]
        + [at.along_b(k) for k in (1, 2, 3)]
        + x_peers(at)
    )


def more_peers(at):
    return all_peers(at) + [at.across(k) for k in (1, 2, 3)]


class Sems:
    def __init__(self, send, recv):
        self.send, self.recv, self.used = send, recv, 0

    def copy(self, src, dst, device):
        index = self.used
        self.used += 1
        made = pltpu.make_async_remote_copy(
            src_ref=src,
            dst_ref=dst,
            send_sem=self.send.at[index],
            recv_sem=self.recv.at[index],
            device_id=device,
            device_id_type=MESH,
        )
        made.start()
        return made


def together(order, *parts, ends=True):
    parts = list(parts)
    for index in order:
        next(parts[index], None)
    while ends and parts:
        for part in list(parts):
            try:
                next(part)
            except StopIteration:
                parts.remove(part)


def rows_of(start, count, multiple):
    return pl.ds(pl.multiple_of(start, multiple), count)


def half_rows(block, half):
    return rows_of(block * OWN + half * HALF, HALF, HALF)


def gather_x(at, sems, out):
    def block(b, half):
        return out.at[half_rows(b, half), :]

    x, r, l = at.x, (at.x + 1) % 4, (at.x + 3) % 4
    c0 = sems.copy(block(x, 0), block(x, 0), at.right)
    c1 = sems.copy(block(x, 1), block(x, 1), at.left)
    yield
    c0.wait_send()
    c2 = sems.copy(block(x, 1), block(x, 1), at.right)
    c1.wait_send()
    c3 = sems.copy(block(x, 0), block(x, 0), at.left)
    yield
    c0.wait_recv()
    c4 = sems.copy(block(l, 0), block(l, 0), at.right)
    yield
    c1.wait_recv()
    c5 = sems.copy(block(r, 1), block(r, 1), at.left)
    yield
    for c in (c2, c3, c4, c5):
        c.wait_recv()
    for c in (c2, c3, c4, c5):
        c.wait_send()


def scatter_x(at, sems, up, buf, tmp, total):
    def block(b, half):
        return up.at[half_rows(b, half), :]

    def value(b, half):
        return up[half_rows(b, half), :].astype(f32)

    x, r, l, o = at.x, (at.x + 1) % 4, (at.x + 3) % 4, (at.x + 2) % 4
    c0 = sems.copy(block(o, 0), buf.at[0], at.right)
    c1 = sems.copy(block(o, 1), buf.at[1], at.left)
    yield
    c0.wait_send()
    c2 = sems.copy(block(r, 1), buf.at[2], at.right)
    c1.wait_send()
    c3 = sems.copy(block(l, 0), buf.at[3], at.left)
    yield
    c0.wait_recv()
    tmp[0] = (value(r, 0) + buf[0].astype(f32)).astype(bf16)
    c4 = sems.copy(tmp.at[0], buf.at[4], at.right)
    yield
    c1.wait_recv()
    tmp[1] = (value(l, 1) + buf[1].astype(f32)).astype(bf16)
    c5 = sems.copy(tmp.at[1], buf.at[5], at.left)
    yield
    for c in (c2, c3, c4, c5):
        c.wait_recv()
    total[0:HALF, :] = value(x, 0) + buf[4].astype(f32) + buf[3].astype(f32)
    total[HALF:OWN, :] = value(x, 1) + buf[2].astype(f32) + buf[5].astype(f32)
    for c in (c2, c3, c4, c5):
        c.wait_send()


def share_squares(at, sems, squares, buf):
    def lanes(x):
        return rows_of(x * OWN, OWN, OWN)

    copies = [
        sems.copy(squares.at[:, lanes((at.x + k) % 4)], buf.at[k - 1], at.along_x(k))
        for k in (1, 2, 3)
    ]
    yield
    for c in copies:
        c.wait_recv()
    buf[3] = squares[:, lanes(at.x)] + buf[0] + buf[1] + buf[2]
    for c in copies:
        c.wait_send()


def share_rows(at, sems, rk):
    copies = [sems.copy(rk.at[at.x], rk.at[at.x], at.along_x(k)) for k in (1, 2, 3)]
    yield
    for c in copies:
        c.wait_recv()
    for c in copies:
        c.wait_send()


def gather_weights(at, sems, shard, met, out):
    mine = rows_of(at.core * HALFW, HALFW, HALFW)

    def block(chip):
        return out.at[rows_of(chip * PAIR, PAIR, PAIR), mine]

    first = sems.copy(shard, met, at.partner)
    yield
    first.wait_recv()
    core = at.core.astype(f32)
    own, theirs = shard[0:ROWS, :].astype(f32), met[0:ROWS, :].astype(f32)
    low = own * (1.0 - core) + theirs * core
    high = own * core + theirs * (1.0 - core)
    out[rows_of(at.chip * PAIR, PAIR, PAIR), :] = jnp.concatenate([low, high], axis=0).astype(bf16)
    along_a = [None] + [sems.copy(block(at.chip), block(at.chip), at.along_a(k)) for k in (1, 2, 3)]
    along_b = []
    passed = []
    for k in range(4):
        if k:
            yield
            along_a[k].wait_recv()
        now = block(at.chip_at((at.a + 4 - k) % 4, at.b))
        for j in (1, 2, 3):
            along_b.append((k, j, sems.copy(now, now, at.along_b(j))))
        if k:
            passed.append(sems.copy(now, now, at.partner))
    for k, j, c in along_b:
        yield
        c.wait_recv()
        now = block(at.chip_at((at.a + 4 - k) % 4, (at.b + 4 - j) % 4))
        passed.append(sems.copy(now, now, at.partner))
    yield
    for c in passed:
        c.wait_recv()
    for c in [first] + along_a[1:] + [c for _, _, c in along_b] + passed:
        c.wait_send()


def scatter_weights(at, sems, grads, out, met, held, got, sums, got_last, final, met_final, xgot):
    mine = rows_of(at.core * HALFW, HALFW, HALFW)
    others = rows_of(at.other * HALFW, HALFW, HALFW)

    def rows(chip):
        return rows_of(chip * PAIR, PAIR, PAIR)

    order = [(j, m) for j in (1, 2, 3, 0) for m in range(4)]
    first = []
    for j, m in order:
        chip = at.partners_chip_at(m, (at.a + j) % 4)
        first.append(sems.copy(grads.at[rows(chip), others], met.at[rows(chip), :], at.partner))
    second = []
    yield
    for (j, m), c in zip(order, first):
        c.wait_recv()
        chip = at.chip_at(m, (at.b + j) % 4)
        both = grads[rows(chip), mine].astype(f32) + met[rows(chip), :].astype(f32)
        held[j, m] = both.astype(bf16)
        if j:
            second.append(sems.copy(held.at[j, m], got.at[j - 1, m], at.along_b(j)))
    yield
    for c in second:
        c.wait_recv()

    def summed(m):
        return (
            held[0, m].astype(f32)
            + got[0, m].astype(f32)
            + got[1, m].astype(f32)
            + got[2, m].astype(f32)
        )

    third = []
    for k in (1, 2, 3):
        sums[k] = summed((at.a + k) % 4).astype(bf16)
        third.append(sems.copy(sums.at[k], got_last.at[k - 1], at.along_a(k)))
    last = summed(at.a)
    yield
    for c in third:
        c.wait_recv()
    final[...] = (
        last
        + got_last[0].astype(f32)
        + got_last[1].astype(f32)
        + got_last[2].astype(f32)
    )
    fourth = sems.copy(final.at[rows_of(at.other * ROWS, ROWS, 8), :], met_final, at.partner)
    fifth = []
    for k in (1, 2, 3):
        index = sems.used
        sems.used += 2
        for extra, core, peer in ((0, at.core, at.along_x(k)), (1, at.other, at.across(k))):
            fifth.append(
                pltpu.make_async_remote_copy(
                    src_ref=final.at[rows_of(core * ROWS, ROWS, 8), 0:384],
                    dst_ref=xgot.at[k - 1],
                    send_sem=sems.send.at[index + extra],
                    recv_sem=sems.recv.at[index],
                    device_id=peer,
                    device_id_type=MESH,
                )
            )

    @pl.when(at.core == 1)
    def _():
        for c in fifth:
            c.start()

    out[:, mine] = final[rows_of(at.core * ROWS, ROWS, 8), :]
    yield
    fourth.wait_recv()
    out[:, others] = met_final[...]
    for c in fifth[::2]:
        c.wait_recv()
    lane = iota((ROWS, 384), 1)
    shared = (lane < 256) | ((lane >= 256 + 66) & (lane < 256 + 106))
    out[:, 768:1152] = out[:, 768:1152] + jnp.where(shared, xgot[0] + xgot[1] + xgot[2], 0.0)

    @pl.when(at.core == 1)
    def _():
        for c in fifth:
            c.wait_send()

    for c in first + second + third + [fourth]:
        c.wait_send()


def sum_everywhere(at, sems, values, held, got):
    held[0] = values[...]
    slot = 0
    stages = [
        [at.partner],
        [at.along_a(k) for k in (1, 2, 3)],
        [at.along_b(k) for k in (1, 2, 3)],
        [at.along_x(k) for k in (1, 2, 3)],
    ]
    for stage, peers in enumerate(stages):
        copies = []
        for peer in peers:
            copies.append(sems.copy(held.at[stage], got.at[slot], peer))
            slot += 1
        yield
        for c in copies:
            c.wait_recv()
        more = got[slot - len(peers)]
        for s in range(slot - len(peers) + 1, slot):
            more = more + got[s]
        if stage == 3:
            more = jnp.where(iota((32, 128), 0) < 16, more, 0.0)
        held[stage + 1] = held[stage] + more
        for c in copies:
            c.wait_send()
    values[...] = held[4]


def row_scale(values):
    return lax.rsqrt(jnp.mean(values * values, axis=-1, keepdims=True) + epsilon)


def put_own(at, out, values):
    out[rows_of(at.x * OWN, OWN, OWN), :] = values


def put_rows(at, rk, r, k):
    row = iota((8, 128), 0)
    rk[at.x] = jnp.where(row == 0, to_row(r), jnp.where(row == 1, to_row(k), 0.0))


def pack_shard(layer, w_zx, w_bc, w_dt, conv_x, conv_bc, gate_gain, w_out, spare, shard):
    spare[...] = jnp.zeros(spare.shape, f32)
    spare[0:LOCAL, 0:ROWS] = w_dt[:, layer, :].astype(f32)
    spare[...] = spare[...].T
    at = LOCAL
    for tap in range(5):
        values = conv_x[layer, tap].astype(f32)
        for e in range(2):
            spare[0:1, at : at + LOCAL] = values[e : e + 1, :]
            at += LOCAL
    for tap in range(5):
        spare[0:1, at : at + 8] = conv_bc[tap].astype(f32)[layer : layer + 1, :]
        at += 8
    values = gate_gain[layer].astype(f32)
    for e in range(2):
        spare[0:1, at : at + LOCAL] = values[e : e + 1, :]
        at += LOCAL
    gates, signals = w_zx[layer, :, 0, :].astype(f32), w_zx[layer, :, 1, :].astype(f32)
    sides = [gates, signals, w_bc[layer].astype(f32), spare[0:ROWS, :], w_out[layer].astype(f32)]
    whole = jnp.concatenate(sides, axis=1)
    below = jnp.zeros((32 - ROWS, WIDE), f32)
    shard[...] = jnp.concatenate([whole, below], axis=0).astype(bf16)


def gate_scale(sqbuf):
    return to_column(lax.rsqrt(sqbuf[3][0:1, :] / DI + epsilon))


def norm_back(gnorm, stream, gain, grad):
    q = row_scale(stream)
    gain_row = jnp.sum(gnorm * stream * q, axis=0, keepdims=True)
    rows = gnorm * gain
    inner = jnp.mean(rows * stream, axis=1, keepdims=True)
    return grad + q * rows - stream * (q * q * q) * inner, gain_row


SCRATCH = {
    "shard0": ((32, WIDE), bf16),
    "shard1": ((32, WIDE), bf16),
    "met0": ((32, WIDE), bf16),
    "met1": ((32, WIDE), bf16),
    "spare": ((128, 128), f32),
    "heads": ((2, 8, 128), f32),
    "weights0": ((D, WIDE), bf16),
    "weights1": ((D, WIDE), bf16),
    "ng0": ((TOK, D), bf16),
    "ng1": ((TOK, D), bf16),
    "gb0": ((TOK, D), bf16),
    "gb1": ((TOK, D), bf16),
    "marks": ((3, TOK, 128), f32),
    "bias": ((TOK, TOK), f32),
    "bias_t": ((TOK, TOK), f32),
    "inner": ((TOK, TOK), f32),
    "dinner": ((TOK, TOK), f32),
    "act": ((TOK, CONV), bf16),
    "xs": ((TOK, UNITS), bf16),
    "d16": ((TOK, UNITS), bf16),
    "mixed": ((TOK, UNITS), bf16),
    "z": ((TOK, UNITS), f32),
    "dsc": ((TOK, UNITS), f32),
    "grads": ((TOK, 1152), bf16),
    "grad_small": ((8, CONV), f32),
    "up": ((TOK, D), bf16),
    "gn": ((TOK, D), bf16),
    "squares": ((8, TOK), f32),
    "tmp": ((2, HALF, D), bf16),
    "total": ((OWN, D), f32),
    "stream1": ((OWN, D), f32),
    "branch0": ((OWN, D), f32),
    "grad0": ((OWN, D), f32),
    "gg1": ((8, 128), f32),
    "held": ((5, 32, 128), f32),
    "got": ((10, 32, 128), f32),
}
for layer_name in "01":
    SCRATCH["proj" + layer_name] = ((TOK, 1152), f32)
    SCRATCH["y" + layer_name] = ((TOK, UNITS), f32)
    SCRATCH["logs" + layer_name] = ((TOK, 128), f32)
    SCRATCH["small" + layer_name] = ((8, CONV), f32)
    SCRATCH["sq" + layer_name] = ((4, 8, 128), f32)
    SCRATCH["rk" + layer_name] = ((4, 8, 128), f32)
    SCRATCH["gw" + layer_name] = ((D, WIDE), bf16)
    SCRATCH["head" + layer_name] = ((8, 128), f32)
    SCRATCH["up_got" + layer_name] = ((6, HALF, D), bf16)
    SCRATCH["gn_got" + layer_name] = ((6, HALF, D), bf16)
SCATTER = [
    ((D, HALFW), bf16),
    ((4, 4, PAIR, HALFW), bf16),
    ((3, 4, PAIR, HALFW), bf16),
    ((4, PAIR, HALFW), bf16),
    ((3, PAIR, HALFW), bf16),
    ((PAIR, HALFW), f32),
    ((ROWS, HALFW), f32),
    ((3, ROWS, 384), f32),
]
for layer_name in "01":
    for part, form in enumerate(SCATTER):
        SCRATCH[f"scatter{layer_name}{part}"] = form
ARGUMENTS = (
    "tokens",
    "gains",
    "cot",
    "step_bias",
    "log_rates",
    "skips",
    "w_zx",
    "w_bc",
    "w_dt",
    "conv_x",
    "conv_bc",
    "gate_gain",
    "w_out",
)
RESULTS = ("block_out", "input_grad", "sum0", "sum1", "values")
COPIES = 208


def whole_kernel(names, *refs):
    a = SimpleNamespace(**dict(zip(names, refs)))
    sources, staged = refs[1:14], [getattr(a, "v_" + name) for name in ARGUMENTS]
    at = Place()
    sems = Sems(a.send, a.recv)
    peers = more_peers(at)
    greet(peers)
    loads = [
        pltpu.make_async_copy(source, target, a.arrived.at[index])
        for index, (source, target) in enumerate(zip(sources, staged))
    ]
    for load in loads:
        load.start()
    for load in loads:
        load.wait()
    tokens, gains, cot, step_bias, log_rates, skips = staged[:6]
    parts = (*staged[6:], a.spare)

    def kept(layer):
        return [getattr(a, name + layer) for name in ("proj", "y", "logs", "small")]

    def forward(layer, ng, weights):
        return forward_steps(
            layer, ng, weights, a.heads, *kept(str(layer)), a.up, a.squares,
            a.marks, a.bias, a.inner, a.act, a.xs,
        )

    def backward(layer, gb, ng, weights, rk, gw, head):
        return backward_steps(
            layer, gb, ng, weights, a.heads, *kept(str(layer)), rk, a.gn, gw, head,
            a.marks, a.bias_t, a.inner, a.dinner, a.act, a.xs, a.d16, a.mixed, a.z, a.dsc,
            a.grads, a.grad_small,
        )

    def scatter(layer, gw, out):
        sets = [getattr(a, f"scatter{layer}{part}") for part in range(len(SCATTER))]
        return scatter_weights(at, sems, gw, out, *sets)

    pack_shard(0, *parts, a.shard0)
    met_all(peers)
    moving = gather_weights(at, sems, a.shard0, a.met0, a.weights0)
    next(moving)
    stream = tokens[...].astype(f32)
    put_own(at, a.ng0, (stream * row_scale(stream) * gains[0:1, :]).astype(bf16))

    def packing():
        pack_shard(1, *parts, a.shard1)
        a.heads[...] = jnp.zeros(a.heads.shape, f32)
        for layer in range(2):
            for row, values in enumerate((step_bias, log_rates, skips)):
                a.heads[layer, row : row + 1, 0:LOCAL] = values[layer : layer + 1, :]
        fill_masks(a.lengths, a.marks, a.bias, a.bias_t)
        put_own(at, a.gb1, cot[...])
        yield

    together([1, 0, 1, 0, 0, 0, 2, 1, 1], moving, gather_x(at, sems, a.ng0), packing())

    moving = gather_weights(at, sems, a.shard1, a.met1, a.weights1)
    next(moving)
    sharing = gather_x(at, sems, a.gb1)
    together(
        [2, 0, 1, 0, 2, 0, 0, 2, 2, 0, 0, 1, 1, 1, 0, 0, 0],
        forward(0, a.ng0, a.weights0),
        moving,
        sharing,
        ends=False,
    )
    column = {}

    def between():
        yield from scatter_x(at, sems, a.up, a.up_got0, a.tmp, a.total)
        column[0] = gate_scale(a.sq0)
        branch = column[0] * a.total[...]
        stream = tokens[...].astype(f32) + branch
        a.branch0[...] = branch
        a.stream1[...] = stream
        put_own(at, a.ng1, (stream * row_scale(stream) * gains[1:2, :]).astype(bf16))
        yield from gather_x(at, sems, a.ng1)

    together(
        [0, 1, 1, 1, 1, 0, 1, 3] + [2] * 6 + [1] + [2] * 6 + [1, 1],
        share_squares(at, sems, a.squares, a.sq0),
        between(),
        moving,
        sharing,
    )

    together([], forward(1, a.ng1, a.weights1))
    back = backward(1, a.gb1, a.ng1, a.weights1, a.rk1, a.gw1, a.head1)
    together(
        [0, 1, 2, 1, 1, 1, 0, 1],
        share_squares(at, sems, a.squares, a.sq1),
        scatter_x(at, sems, a.up, a.up_got1, a.tmp, a.total),
        back,
        ends=False,
    )
    r = gate_scale(a.sq1)
    branch = r * a.total[...]
    a.block_out[...] = (a.stream1[...] + branch).astype(bf16)
    dots = jnp.sum(cot[...].astype(f32) * branch, axis=1, keepdims=True)
    put_rows(at, a.rk1, r, r * r * dots / DI)
    together([0, 1, 0], share_rows(at, sems, a.rk1), back, ends=False)
    together([0] * 9, back, ends=False)

    def along():
        yield from scatter_x(at, sems, a.gn, a.gn_got1, a.tmp, a.total)
        grad, gain_row = norm_back(
            a.total[...], a.stream1[...], gains[1:2, :], cot[...].astype(f32)
        )
        low = grad.astype(bf16)
        put_own(at, a.gb0, low)
        sharing = gather_x(at, sems, a.gb0)
        next(sharing)
        a.grad0[...] = grad
        dots = jnp.sum(low.astype(f32) * a.branch0[...], axis=1, keepdims=True)
        put_rows(at, a.rk0, column[0], column[0] * column[0] * dots / DI)
        rows = share_rows(at, sems, a.rk0)
        next(rows)
        for c in range(6):
            a.gg1[c : c + 1, :] = gain_row[:, c * 128 : c * 128 + 128]
        yield
        yield from sharing
        yield from rows

    earlier = scatter(1, a.gw1, a.sum1)
    last = backward(0, a.gb0, a.ng0, a.weights0, a.rk0, a.gw0, a.head0)
    together(
        [0, 1, 3, 0, 2, 0, 0, 0, 3, 0, 0, 0, 0],
        along(),
        back,
        last,
        earlier,
        ends=False,
    )
    together([0, 0, 0, 1, 0, 0, 1, 0, 0, 0, 1, 0, 0], last, earlier, ends=False)

    def final():
        yield from scatter_x(at, sems, a.gn, a.gn_got0, a.tmp, a.total)
        grad, gain_row = norm_back(
            a.total[...], tokens[...].astype(f32), gains[0:1, :], a.grad0[...]
        )
        a.input_grad[...] = grad
        a.values[...] = jnp.zeros(a.values.shape, f32)
        for c in range(6):
            a.values[c : c + 1, :] = gain_row[:, c * 128 : c * 128 + 128]
        a.values[6:12, :] = a.gg1[0:6, :]
        a.values[16:24, :] = a.head0[...]
        a.values[24:32, :] = a.head1[...]
        yield from sum_everywhere(at, sems, a.values, a.held, a.got)

    together(
        [0, 1, 2, 0, 2, 0, 0, 0, 2, 0, 2, 0, 2, 0],
        final(),
        last,
        scatter(0, a.gw0, a.sum0),
    )


def finish_kernel(
    sum0, sum1, values, block_in, grad_in,
    block_out, input_grad, norm_gain, zx, bc, dt, conv_x, conv_bc, a_log, dt_bias, d_skip, gate_gain, w_out,
):
    block_out[...] = block_in[...]
    input_grad[...] = grad_in[...]
    for layer, total in enumerate((sum0, sum1)):
        for c in range(6):
            norm_gain[layer : layer + 1, c * 128 : c * 128 + 128] = values[
                layer * 6 + c : layer * 6 + c + 1, :
            ]
        row = 16 + 8 * layer
        for k, out in enumerate((a_log, dt_bias, d_skip)):
            out[layer : layer + 1, :] = values[row + k : row + k + 1, 0:LOCAL]
        zx[layer, :, 0, :] = total[:, 0:UNITS]
        zx[layer, :, 1, :] = total[:, UNITS:768]
        bc[layer] = total[:, 768:1024]
        w_out[layer] = total[:, 1152:]
        spread = total[:, 1024:1152]
        wide = jnp.concatenate([spread, jnp.zeros((128 - ROWS, 128), f32)], axis=0).T
        dt[:, layer, :] = wide[0:LOCAL, 0:ROWS]
        small = total[0:1, 1024:1152]
        at = LOCAL
        for tap in range(5):
            for e in range(2):
                conv_x[layer, tap, e : e + 1, :] = small[:, at : at + LOCAL]
                at += LOCAL
        for tap in range(5):
            conv_bc[tap, layer : layer + 1, :] = small[:, at : at + 8]
            at += 8
        for e in range(2):
            gate_gain[layer, e : e + 1, :] = small[:, at : at + LOCAL]
            at += LOCAL


def body(
    tokens,
    lengths,
    norm_gain,
    w_zx,
    w_bc,
    w_dt,
    conv_x,
    conv_bc,
    a_log,
    dt_bias,
    d_skip,
    gate_gain,
    w_out,
    cotangent,
):
    arguments = (
        tokens,
        norm_gain,
        cotangent,
        dt_bias,
        a_log,
        d_skip,
        w_zx,
        w_bc,
        w_dt.transpose(2, 0, 1),
        conv_x.swapaxes(2, 3),
        conv_bc.swapaxes(0, 1),
        gate_gain.swapaxes(1, 2),
        w_out.swapaxes(1, 2),
    )
    results = [
        shaped((OWN, D), bf16),
        shaped((OWN, D)),
        shaped((ROWS, WIDE)),
        shaped((ROWS, WIDE)),
        shaped((32, 128)),
    ]
    names = ["lengths", *ARGUMENTS, *RESULTS, *("v_" + name for name in ARGUMENTS), *SCRATCH]
    names += ["arrived", "send", "recv"]
    block_out, input_grad, sum0, sum1, values = pl.pallas_call(
        functools.partial(whole_kernel, names),
        out_shape=results,
        in_specs=[pl.BlockSpec(memory_space=pltpu.SMEM)]
        + [pl.BlockSpec(memory_space=pltpu.HBM)] * len(arguments),
        out_specs=[VM] * len(results),
        scratch_shapes=[pltpu.VMEM(argument.shape, argument.dtype) for argument in arguments]
        + [pltpu.VMEM(shape, kind) for shape, kind in SCRATCH.values()]
        + [
            pltpu.SemaphoreType.DMA((len(arguments),)),
            pltpu.SemaphoreType.DMA((COPIES,)),
            pltpu.SemaphoreType.DMA((COPIES,)),
        ],
        compiler_params=pltpu.CompilerParams(
            collective_id=0, has_side_effects=True, vmem_limit_bytes=LIMIT
        ),
    )(lengths, *arguments)
    outs = pl.pallas_call(
        finish_kernel,
        out_shape=[
            shaped((OWN, D), bf16),
            shaped((OWN, D)),
            shaped((2, D)),
            shaped((2, ROWS, 2, UNITS)),
            shaped((2, ROWS, 256)),
            shaped((LOCAL, 2, ROWS)),
            shaped((2, 5, 2, LOCAL)),
            shaped((5, 2, 8)),
            shaped((2, LOCAL)),
            shaped((2, LOCAL)),
            shaped((2, LOCAL)),
            shaped((2, 2, LOCAL)),
            shaped((2, ROWS, UNITS)),
        ],
        in_specs=[VM] * 5,
        out_specs=[VM] * 13,
        compiler_params=pltpu.CompilerParams(vmem_limit_bytes=LIMIT),
    )(sum0, sum1, values, block_out, input_grad)
    block_out, input_grad, g_norm, g_zx, g_bc, g_dt, g_cx, g_cb, g_a, g_b, g_d, g_gate, g_out = outs
    return (
        block_out,
        input_grad,
        g_norm,
        g_zx,
        g_bc,
        g_dt.transpose(1, 2, 0),
        g_cx.swapaxes(2, 3),
        g_cb.swapaxes(0, 1),
        g_a,
        g_b,
        g_d,
        g_gate.swapaxes(1, 2),
        g_out.swapaxes(1, 2),
    )


def solution(mesh):
    return jax.shard_map(
        body,
        mesh=mesh,
        in_specs=(
            P(("dp", "tensor"), None),
            P("dp", None),
            P(),
            P(None, "dp", None, "tensor"),
            P(None, "dp", None),
            P(None, "dp", "tensor"),
            P(None, None, "tensor", "dp"),
            P(None, None, "dp"),
            P(None, "tensor"),
            P(None, "tensor"),
            P(None, "tensor"),
            P(None, "tensor", "dp"),
            P(None, "tensor", "dp"),
            P(("dp", "tensor"), None),
        ),
        out_specs=(
            P(("dp", "tensor"), None),
            P(("dp", "tensor"), None),
            P(),
            P(None, "dp", None, "tensor"),
            P(None, "dp", None),
            P(None, "dp", "tensor"),
            P(None, None, "tensor", "dp"),
            P(None, None, "dp"),
            P(None, "tensor"),
            P(None, "tensor"),
            P(None, "tensor"),
            P(None, "tensor", "dp"),
            P(None, "tensor", "dp"),
        ),
        check_vma=False,
    )
```

```python
import functools
from types import SimpleNamespace

import jax
import jax.numpy as jnp
from jax import lax
from jax.experimental import pallas as pl
from jax.experimental.pallas import tpu as pltpu
from jax.sharding import PartitionSpec as P

D = 768
HEADS = 24
DI = 1536
LOCAL = 6
UNITS = 384
CONV = 640
TOK = 512
OWN = 128
HALF = 64
QUARTER = 32
ROWS = 24
PAIR = 48
WIDE = 1536
HALFW = 768
MESH = pl.DeviceIdType.MESH
epsilon = 1e-05
highest = lax.Precision.HIGHEST
f32 = jnp.float32
bf16 = jnp.bfloat16
FAR = -1e30
LIMIT = 62 * 1024 * 1024
VM = pl.BlockSpec(memory_space=pltpu.VMEM)


def nn(a, b, precision=None):
    return lax.dot_general(
        a, b, (((1,), (0,)), ((), ())), precision=precision, preferred_element_type=f32
    )


def nt(a, b, precision=None):
    return lax.dot_general(
        a, b, (((1,), (1,)), ((), ())), precision=precision, preferred_element_type=f32
    )


def tn(a, b, precision=None):
    return lax.dot_general(
        a, b, (((0,), (0,)), ((), ())), precision=precision, preferred_element_type=f32
    )


def in_parts(values, count):
    parts = []
    for _ in range(count):
        part = values.astype(bf16)
        parts.append(part)
        values = values - part.astype(f32)
    return parts


def sum_left(op, values, ones, count):
    return sum(op(part, ones) for part in in_parts(values, count))


def sum_right(op, ones, values, count):
    return sum(op(ones, part) for part in in_parts(values, count))


def iota(shape, dim):
    return lax.broadcasted_iota(jnp.int32, shape, dim)


def softplus(v):
    return jnp.maximum(v, 0.0) + jnp.log1p(jnp.exp(-jnp.abs(v)))


def one_hot(condition, kind=f32):
    return jnp.where(condition, 1.0, 0.0).astype(kind)


def head_spread():
    return one_hot((iota((128, UNITS), 1) >> 6) == iota((128, UNITS), 0), bf16)


def to_row(column):
    eye = iota((128, 128), 0) == iota((128, 128), 1)
    return jnp.sum(jnp.where(eye, column, 0.0), axis=0, keepdims=True)


def to_column(row):
    eye = iota((128, 128), 0) == iota((128, 128), 1)
    return jnp.sum(jnp.where(eye, row, 0.0), axis=1, keepdims=True)


def small_lanes(tap, width, first):
    unit = iota((width, 128), 0)
    lane = iota((width, 128), 1)
    if width == UNITS:
        place = 6 + first + tap * 12 + (unit & 1) * 6 + (unit >> 6)
    else:
        place = 6 + first + tap * 8 + (unit & 7)
    return one_hot(lane == place, bf16)


def small_owner(width):
    unit = iota((32, width), 1)
    owner = (unit & 63) >> 1 if width == UNITS else unit >> 3
    return one_hot(owner == iota((32, width), 0))


SMALLS = (
    [(tap, UNITS, 0, tap, 0) for tap in range(5)]
    + [(tap, 256, 60, tap, UNITS) for tap in range(5)]
    + [(0, UNITS, 100, 5, 0)]
)


def placing():
    return one_hot(iota((D, 32), 0) == iota((D, 32), 1) * ROWS, bf16)


def segment_starts(lengths, position):
    first = lengths[0, 0]
    second = first + lengths[0, 1]
    return jnp.where(position >= second, second, jnp.where(position >= first, first, 0))


def fill_masks(lengths, marks, bias, bias_t):
    position = iota((TOK, 128), 0)
    since = position - segment_starts(lengths, position)
    for s in (1, 2, 3):
        marks[s - 1] = one_hot(since >= s)
    for b in range(4):
        rows = slice(b * 128, b * 128 + 128)
        here, there = iota((128, TOK), 0) + b * 128, iota((128, TOK), 1)
        linked = (there <= here) & (there >= segment_starts(lengths, here))
        bias[rows, :] = jnp.where(linked, 0.0, FAR)
        linked = (here <= there) & (here >= segment_starts(lengths, there))
        bias_t[rows, :] = jnp.where(linked, 0.0, FAR)


def forward_steps(
    layer, ng, weights, heads_all,
    proj, kept_y, logs, smalls, up, squares,
    marks, bias, inner, act, xs,
):
    heads = heads_all.at[layer]
    proj[...] = nn(ng[...], weights[:, :1152])
    yield
    packed = tn(placing(), weights[:, 1024:1152]).astype(bf16)
    smalls[...] = jnp.zeros(smalls.shape, f32)
    for tap, width, first, row, start in SMALLS:
        spread = nt(packed, small_lanes(tap, width, first)) * small_owner(width)
        smalls[row : row + 1, start : start + width] = jnp.sum(spread, axis=0, keepdims=True)
    yield
    lane = iota((TOK, 128), 1)
    steps = jnp.where(lane < LOCAL, softplus(proj[:, 1024:1152] + heads[0:1, :]), 0.0)
    rates = jnp.where(iota((1, 128), 1) < LOCAL, -jnp.exp(heads[1:2, :]), 0.0)
    log_now = sum_right(nn, one_hot(bias[...] == 0.0, bf16), steps * rates, 3)
    logs[...] = log_now
    log_t = log_now.T
    for c in range(0, CONV, 128):
        cols = slice(c, c + 128)
        v = proj[:, UNITS + c : UNITS + c + 128]
        y = smalls[4:5, cols] + smalls[3:4, cols] * v
        for s in (1, 2, 3):
            y = y + smalls[3 - s : 4 - s, cols] * (marks[s - 1] * pltpu.roll(v, s, 0))
        act[:, cols] = (y * jax.nn.sigmoid(y)).astype(bf16)
    yield
    spread_heads = head_spread()
    skip_row = sum_left(nn, heads[...], spread_heads, 3)[2:3, :]
    xs[...] = (act[:, :UNITS].astype(f32) * sum_left(nn, steps, spread_heads, 3)).astype(bf16)
    inner[...] = nt(act[:, 512:640], act[:, 384:512])
    yield
    for ib in range(4):
        rows = slice(ib * 128, ib * 128 + 128)
        n = ib * 128 + 128
        for p in range(3):
            outs = []
            for h in (2 * p, 2 * p + 1):
                spread = log_now[rows, h : h + 1] - log_t[h : h + 1, :n] + bias[rows, :n]
                g = (inner[rows, :n] * jnp.exp(spread)).astype(bf16)
                outs.append(nn(g, xs[:n, p * 128 : p * 128 + 128]))
            kept_y[rows, p * 128 : p * 128 + 128] = jnp.where(
                iota((128, 128), 1) < 64, outs[0], outs[1]
            )
        yield
    total = jnp.zeros((TOK, 128), f32)
    for p in range(3):
        cols = slice(p * 128, p * 128 + 128)
        gate = proj[:, cols]
        scanned = kept_y[:, cols] + skip_row[:, cols] * act[:, cols].astype(f32)
        gated = scanned * (gate * jax.nn.sigmoid(gate))
        total = total + gated * gated
        xs[:, cols] = (gated * smalls[5:6, cols]).astype(bf16)
    squares[...] = sum_right(nt, jnp.ones((8, 128), bf16), total, 3)
    up[...] = nt(xs[...], weights[:, 1152:]).astype(bf16)


def backward_steps(
    layer,
    gb,
    ng,
    weights,
    heads_all,
    proj,
    kept_y,
    logs,
    smalls,
    rk,
    gn,
    gw,
    head_out,
    marks,
    bias,
    inner,
    dinner,
    act,
    xs,
    d16,
    mixed,
    z,
    dsc,
    grads,
    grad_small,
):
    heads = heads_all.at[layer]
    lane = iota((TOK, 128), 1)
    step_in = proj[:, 1024:1152] + heads[0:1, :]
    steps = jnp.where(lane < LOCAL, softplus(step_in), 0.0)
    rates = jnp.where(iota((1, 128), 1) < LOCAL, -jnp.exp(heads[1:2, :]), 0.0)
    log_now = logs[...]
    log_t = log_now.T
    spread_heads = head_spread()
    skip_row = sum_left(nn, heads[...], spread_heads, 3)[2:3, :]
    step_wide = sum_left(nn, steps, spread_heads, 3)

    def conv_of(c):
        cols = slice(c, c + 128)
        v = proj[:, UNITS + c : UNITS + c + 128]
        y = smalls[4:5, cols] + smalls[3:4, cols] * v
        for s in (1, 2, 3):
            y = y + smalls[3 - s : 4 - s, cols] * (marks[s - 1] * pltpu.roll(v, s, 0))
        return v, y

    for c in range(0, CONV, 128):
        v, y = conv_of(c)
        act[:, c : c + 128] = (y * jax.nn.sigmoid(y)).astype(bf16)
    xs[...] = (act[:, :UNITS].astype(f32) * step_wide).astype(bf16)
    yield
    z[...] = nn(gb[...], weights[:, 1152:])
    yield
    r = jnp.concatenate([to_column(rk[b, 0:1, :]) for b in range(4)], axis=0)
    k = jnp.concatenate([to_column(rk[b, 1:2, :]) for b in range(4)], axis=0)
    head_rows = jnp.zeros((8, 128), f32)
    grad_small[...] = jnp.zeros(grad_small.shape, f32)
    skip_parts = []
    for p in range(3):
        cols = slice(p * 128, p * 128 + 128)
        gate = proj[:, cols]
        sig = jax.nn.sigmoid(gate)
        x = act[:, cols].astype(f32)
        scanned = kept_y[:, cols] + skip_row[:, cols] * x
        gated = scanned * (gate * sig)
        gain = smalls[5:6, cols]
        gm = z[:, cols]
        scaled = gated * r
        mixed[:, cols] = (scaled * gain).astype(bf16)
        grad_small[5:6, cols] = jnp.sum(gm * scaled, axis=0, keepdims=True)
        gg = r * (gm * gain) - gated * k
        ds_now = gg * (gate * sig)
        grads[:, cols] = (gg * scanned * sig * (1.0 + gate * (1.0 - sig))).astype(bf16)
        dsc[:, cols] = ds_now
        d16[:, cols] = ds_now.astype(bf16)
        skip_parts.append(jnp.sum(ds_now * x, axis=0, keepdims=True))
    yield
    gw[:, 1152:] = tn(gb[...], mixed[...]).astype(bf16)
    gw[:, :UNITS] = tn(ng[...], grads[:, :UNITS]).astype(bf16)
    yield
    inner[...] = nt(act[:, 384:512], act[:, 512:640])
    dinner[...] = jnp.zeros(dinner.shape, f32)
    low_lanes = iota((128, 128), 1) < 64
    for jb in range(4):
        i0 = jb * 128
        rows = slice(i0, i0 + 128)
        for p in range(3):
            cols = slice(p * 128, p * 128 + 128)
            outs = []
            xp = xs[rows, cols]
            dp = d16[i0:, cols]
            for h in (2 * p, 2 * p + 1):
                spread = log_t[h : h + 1, i0:] - log_now[rows, h : h + 1] + bias[rows, i0:]
                e = jnp.exp(spread)
                outs.append(nn((inner[rows, i0:] * e).astype(bf16), dp))
                keep = low_lanes if h == 2 * p else jnp.logical_not(low_lanes)
                xh = jnp.where(keep, xp.astype(f32), 0.0).astype(bf16)
                dinner[rows, i0:] = dinner[rows, i0:] + e * nt(xh, dp)
            z[rows, cols] = jnp.where(low_lanes, outs[0], outs[1])
        yield
    x32 = act[:, :UNITS].astype(f32)
    zz = z[...]
    twice = d16[...].astype(f32) * kept_y[...] - xs[...].astype(f32) * zz
    dlog = sum_left(nt, twice, spread_heads, 2)
    dstep = sum_left(nt, x32 * zz, spread_heads, 2)
    da = sum_right(nn, one_hot(bias[...] == 0.0, bf16), dlog, 3)
    dstep = dstep + da * rates
    ddt = jnp.where(lane < LOCAL, dstep * jax.nn.sigmoid(step_in), 0.0)
    skip_all = jnp.concatenate(skip_parts, axis=1)
    skip_heads = sum_left(nt, jnp.broadcast_to(skip_all, (8, UNITS)), spread_heads, 3)
    row = iota((8, 128), 0)
    a_row = jnp.sum(da * steps, axis=0, keepdims=True) * rates
    b_row = jnp.sum(ddt, axis=0, keepdims=True)
    head_out[...] = jnp.where(
        row == 0, a_row, jnp.where(row == 1, b_row, jnp.where(row == 2, skip_heads, 0.0))
    )
    grads[:, 1024:1152] = ddt.astype(bf16)
    yield
    din = dinner[...].astype(bf16)
    grad_b = nn(din, act[:, 512:640])
    grad_c = tn(din, act[:, 384:512])
    for c in range(0, CONV, 128):
        cols = slice(c, c + 128)
        if c < UNITS:
            dact = step_wide[:, cols] * z[:, cols] + skip_row[:, cols] * dsc[:, cols]
        else:
            dact = grad_b if c == UNITS else grad_c
        v, y = conv_of(c)
        sig = jax.nn.sigmoid(y)
        dy = dact * sig * (1.0 + y * (1.0 - sig))
        grad_small[4:5, cols] = jnp.sum(dy, axis=0, keepdims=True)
        grad_small[3:4, cols] = jnp.sum(dy * v, axis=0, keepdims=True)
        dv = smalls[3:4, cols] * dy
        for s in (1, 2, 3):
            masked = marks[s - 1] * dy
            grad_small[3 - s : 4 - s, cols] = jnp.sum(
                masked * pltpu.roll(v, s, 0), axis=0, keepdims=True
            )
            dv = dv + smalls[3 - s : 4 - s, cols] * pltpu.roll(masked, TOK - s, 0)
        grads[:, UNITS + c : UNITS + c + 128] = dv.astype(bf16)
    yield
    gn[...] = nt(grads[...], weights[:, :1152]).astype(bf16)
    yield
    gw[:, UNITS:1024] = tn(ng[...], grads[:, UNITS:1024]).astype(bf16)
    packed = jnp.zeros((32, 128), f32)
    for tap, width, first, row_at, start in SMALLS:
        values = (
            small_owner(width) * grad_small[row_at : row_at + 1, start : start + width]
        ).astype(bf16)
        packed = packed + nn(values, small_lanes(tap, width, first))
    last = tn(ng[...], grads[:, 1024:1152]) + nn(placing(), packed.astype(bf16))
    gw[:, 1024:1152] = last.astype(bf16)


VM = pl.BlockSpec(memory_space=pltpu.VMEM)


def shaped(shape, kind=f32):
    return jax.ShapeDtypeStruct(shape, kind)


class Place:
    def __init__(self):
        self.dp = lax.axis_index("dp")
        self.x = lax.axis_index("tensor")
        self.core = self.dp % 2
        self.other = 1 - self.core
        self.chip = self.dp // 2
        y, z = self.chip % 4, self.chip // 4
        self.a = self.other * y + self.core * z
        self.b = self.other * z + self.core * y
        self.partner = (self.chip * 2 + self.other, self.x)
        self.right = (self.dp, (self.x + 1) % 4)
        self.left = (self.dp, (self.x + 3) % 4)

    def chip_at(self, a, b):
        return self.other * (b * 4 + a) + self.core * (a * 4 + b)

    def partners_chip_at(self, a, b):
        return self.core * (b * 4 + a) + self.other * (a * 4 + b)

    def along_a(self, k):
        return (self.chip_at((self.a + k) % 4, self.b) * 2 + self.core, self.x)

    def along_b(self, k):
        return (self.chip_at(self.a, (self.b + k) % 4) * 2 + self.core, self.x)

    def across(self, k):
        return (self.chip * 2 + self.other, (self.x + k) % 4)

    def along_x(self, k):
        return (self.dp, (self.x + k) % 4)


def greet(peers):
    barrier = pltpu.get_barrier_semaphore()
    for peer in peers:
        pl.semaphore_signal(barrier, inc=1, device_id=peer, device_id_type=MESH)


def met_all(peers):
    pl.semaphore_wait(pltpu.get_barrier_semaphore(), len(peers))


def x_peers(at):
    return [at.along_x(k) for k in (1, 2, 3)]


def all_peers(at):
    return (
        [at.partner]
        + [at.along_a(k) for k in (1, 2, 3)]
        + [at.along_b(k) for k in (1, 2, 3)]
        + x_peers(at)
    )


def more_peers(at):
    return all_peers(at) + [at.across(k) for k in (1, 2, 3)]


class Sems:
    def __init__(self, send, recv):
        self.send, self.recv, self.used = send, recv, 0

    def copy(self, src, dst, device):
        index = self.used
        self.used += 1
        made = pltpu.make_async_remote_copy(
            src_ref=src,
            dst_ref=dst,
            send_sem=self.send.at[index],
            recv_sem=self.recv.at[index],
            device_id=device,
            device_id_type=MESH,
        )
        made.start()
        return made


def together(order, *parts, ends=True):
    parts = list(parts)
    for index in order:
        next(parts[index], None)
    while ends and parts:
        for part in list(parts):
            try:
                next(part)
            except StopIteration:
                parts.remove(part)


def rows_of(start, count, multiple):
    return pl.ds(pl.multiple_of(start, multiple), count)


def half_rows(block, part, half):
    return rows_of(block * OWN + part * HALF + half * QUARTER, QUARTER, QUARTER)


def gather_x(at, sems, out, part):
    def block(b, half):
        return out.at[half_rows(b, part, half), :]

    x, r, l = at.x, (at.x + 1) % 4, (at.x + 3) % 4
    c0 = sems.copy(block(x, 0), block(x, 0), at.right)
    c1 = sems.copy(block(x, 1), block(x, 1), at.left)
    yield
    c0.wait_send()
    c2 = sems.copy(block(x, 1), block(x, 1), at.right)
    c1.wait_send()
    c3 = sems.copy(block(x, 0), block(x, 0), at.left)
    yield
    c0.wait_recv()
    c4 = sems.copy(block(l, 0), block(l, 0), at.right)
    c1.wait_recv()
    c5 = sems.copy(block(r, 1), block(r, 1), at.left)
    yield
    for c in (c2, c3, c4, c5):
        c.wait_recv()
    for c in (c2, c3, c4, c5):
        c.wait_send()


def scatter_x(at, sems, up, buf, tmp, total, part):
    def block(b, half):
        return up.at[half_rows(b, part, half), :]

    def value(b, half):
        return up[half_rows(b, part, half), :].astype(f32)

    def received(slot):
        return buf[part, slot].astype(f32)

    x, r, l, o = at.x, (at.x + 1) % 4, (at.x + 3) % 4, (at.x + 2) % 4
    c0 = sems.copy(block(o, 0), buf.at[part, 0], at.right)
    c1 = sems.copy(block(o, 1), buf.at[part, 1], at.left)
    yield
    c0.wait_send()
    c2 = sems.copy(block(r, 1), buf.at[part, 2], at.right)
    c1.wait_send()
    c3 = sems.copy(block(l, 0), buf.at[part, 3], at.left)
    yield
    c0.wait_recv()
    tmp[part, 0] = (value(r, 0) + received(0)).astype(bf16)
    c4 = sems.copy(tmp.at[part, 0], buf.at[part, 4], at.right)
    c1.wait_recv()
    tmp[part, 1] = (value(l, 1) + received(1)).astype(bf16)
    c5 = sems.copy(tmp.at[part, 1], buf.at[part, 5], at.left)
    yield
    for c in (c2, c3, c4, c5):
        c.wait_recv()
    first = part * HALF
    total[first : first + QUARTER, :] = value(x, 0) + received(4) + received(3)
    total[first + QUARTER : first + HALF, :] = value(x, 1) + received(2) + received(5)
    for c in (c2, c3, c4, c5):
        c.wait_send()


def share_squares(at, sems, squares, buf):
    def lanes(x):
        return rows_of(x * OWN, OWN, OWN)

    copies = [
        sems.copy(squares.at[:, lanes((at.x + k) % 4)], buf.at[k - 1], at.along_x(k))
        for k in (1, 2, 3)
    ]
    yield
    for c in copies:
        c.wait_recv()
    buf[3] = squares[:, lanes(at.x)] + buf[0] + buf[1] + buf[2]
    for c in copies:
        c.wait_send()


def share_rows(at, sems, rk):
    copies = [sems.copy(rk.at[at.x], rk.at[at.x], at.along_x(k)) for k in (1, 2, 3)]
    yield
    for c in copies:
        c.wait_recv()
    for c in copies:
        c.wait_send()


def gather_weights(at, sems, shard, met, out):
    mine = rows_of(at.core * HALFW, HALFW, HALFW)

    def block(chip):
        return out.at[rows_of(chip * PAIR, PAIR, PAIR), mine]

    first = sems.copy(shard, met, at.partner)
    yield
    first.wait_recv()
    core = at.core.astype(f32)
    own, theirs = shard[0:ROWS, :].astype(f32), met[0:ROWS, :].astype(f32)
    low = own * (1.0 - core) + theirs * core
    high = own * core + theirs * (1.0 - core)
    out[rows_of(at.chip * PAIR, PAIR, PAIR), :] = jnp.concatenate([low, high], axis=0).astype(bf16)
    along_a = [None] + [sems.copy(block(at.chip), block(at.chip), at.along_a(k)) for k in (1, 2, 3)]
    along_b = []
    passed = []
    for k in range(4):
        if k:
            yield
            along_a[k].wait_recv()
        now = block(at.chip_at((at.a + 4 - k) % 4, at.b))
        for j in (1, 2, 3):
            along_b.append((k, j, sems.copy(now, now, at.along_b(j))))
        if k:
            passed.append(sems.copy(now, now, at.partner))
    for k, j, c in along_b:
        yield
        c.wait_recv()
        now = block(at.chip_at((at.a + 4 - k) % 4, (at.b + 4 - j) % 4))
        passed.append(sems.copy(now, now, at.partner))
    yield
    for c in passed:
        c.wait_recv()
    for c in [first] + along_a[1:] + [c for _, _, c in along_b] + passed:
        c.wait_send()


def scatter_weights(
    at, sems, late, grads, out, met, held, got, sums, got_last, final, met_final, xgot
):
    if late:
        mine, others = (rows_of(UNITS + core * UNITS, UNITS, 128) for core in (at.core, at.other))
    else:
        mine, others = (rows_of(core * 1152, UNITS, 128) for core in (at.core, at.other))

    def rows(chip):
        return rows_of(chip * PAIR, PAIR, PAIR)

    order = [(j, m) for j in (1, 2, 3, 0) for m in range(4)]
    first = []
    for j, m in order:
        chip = at.partners_chip_at(m, (at.a + j) % 4)
        first.append(sems.copy(grads.at[rows(chip), others], met.at[rows(chip), :], at.partner))
    second = []
    yield
    for (j, m), c in zip(order, first):
        c.wait_recv()
        chip = at.chip_at(m, (at.b + j) % 4)
        both = grads[rows(chip), mine].astype(f32) + met[rows(chip), :].astype(f32)
        held[j, m] = both.astype(bf16)
        if j:
            second.append(sems.copy(held.at[j, m], got.at[j - 1, m], at.along_b(j)))
    yield
    for c in second:
        c.wait_recv()

    def summed(m):
        return (
            held[0, m].astype(f32)
            + got[0, m].astype(f32)
            + got[1, m].astype(f32)
            + got[2, m].astype(f32)
        )

    third = []
    for k in (1, 2, 3):
        sums[k] = summed((at.a + k) % 4).astype(bf16)
        third.append(sems.copy(sums.at[k], got_last.at[k - 1], at.along_a(k)))
    last = summed(at.a)
    yield
    for c in third:
        c.wait_recv()
    final[...] = (
        last
        + got_last[0].astype(f32)
        + got_last[1].astype(f32)
        + got_last[2].astype(f32)
    )
    fourth = sems.copy(final.at[rows_of(at.other * ROWS, ROWS, 8), :], met_final, at.partner)
    fifth = []
    for k in (1, 2, 3) if late else ():
        index = sems.used
        sems.used += 2
        for extra, core, peer in ((0, at.core, at.along_x(k)), (1, at.other, at.across(k))):
            fifth.append(
                pltpu.make_async_remote_copy(
                    src_ref=final.at[rows_of(core * ROWS, ROWS, 8), :],
                    dst_ref=xgot.at[k - 1],
                    send_sem=sems.send.at[index + extra],
                    recv_sem=sems.recv.at[index],
                    device_id=peer,
                    device_id_type=MESH,
                )
            )

    if late:

        @pl.when(at.core == 1)
        def _():
            for c in fifth:
                c.start()

    out[:, mine] = final[rows_of(at.core * ROWS, ROWS, 8), :]
    yield
    fourth.wait_recv()
    out[:, others] = met_final[...]
    if late:
        for c in fifth[::2]:
            c.wait_recv()
        lane = iota((ROWS, 384), 1)
        shared = (lane < 256) | ((lane >= 256 + 66) & (lane < 256 + 106))
        more = jnp.where(shared, xgot[0] + xgot[1] + xgot[2], 0.0)
        out[:, 768:1152] = out[:, 768:1152] + more

        @pl.when(at.core == 1)
        def _():
            for c in fifth:
                c.wait_send()

    for c in first + second + third + [fourth]:
        c.wait_send()


def sum_everywhere(at, sems, values, held, got):
    held[0] = values[...]
    stages = [
        [at.partner] + [at.along_x(k) for k in (1, 2, 3)] + [at.across(k) for k in (1, 2, 3)],
        [at.along_a(k) for k in (1, 2, 3)],
        [at.along_b(k) for k in (1, 2, 3)],
    ]
    slot = 0
    for stage, peers in enumerate(stages):
        copies = []
        for peer in peers:
            copies.append(sems.copy(held.at[stage], got.at[slot], peer))
            slot += 1
        yield
        for c in copies:
            c.wait_recv()
        first = slot - len(peers)
        if stage == 0:
            more = sum(got[n] for n in range(2, slot)) + got[1]
            more = got[0] + jnp.where(iota((32, 128), 0) < 16, more, 0.0)
        else:
            more = got[first] + got[first + 1] + got[first + 2]
        held[stage + 1] = held[stage] + more
        for c in copies:
            c.wait_send()
    values[...] = held[3]


def row_scale(values):
    return lax.rsqrt(jnp.mean(values * values, axis=-1, keepdims=True) + epsilon)


def put_own(at, out, values, part=None):
    if part is None:
        out[rows_of(at.x * OWN, OWN, OWN), :] = values
    else:
        out[rows_of(at.x * OWN + part * HALF, HALF, HALF), :] = values


def put_rows(at, rk, r, k):
    row = iota((8, 128), 0)
    rk[at.x] = jnp.where(row == 0, to_row(r), jnp.where(row == 1, to_row(k), 0.0))


def pack_shard(layer, w_zx, w_bc, w_dt, conv_x, conv_bc, gate_gain, w_out, spare, shard):
    spare[...] = jnp.zeros(spare.shape, f32)
    spare[0:LOCAL, 0:ROWS] = w_dt[:, layer, :].astype(f32)
    spare[...] = spare[...].T
    at = LOCAL
    for tap in range(5):
        values = conv_x[layer, tap].astype(f32)
        for e in range(2):
            spare[0:1, at : at + LOCAL] = values[e : e + 1, :]
            at += LOCAL
    for tap in range(5):
        spare[0:1, at : at + 8] = conv_bc[tap].astype(f32)[layer : layer + 1, :]
        at += 8
    values = gate_gain[layer].astype(f32)
    for e in range(2):
        spare[0:1, at : at + LOCAL] = values[e : e + 1, :]
        at += LOCAL
    gates, signals = w_zx[layer, :, 0, :].astype(f32), w_zx[layer, :, 1, :].astype(f32)
    sides = [gates, signals, w_bc[layer].astype(f32), spare[0:ROWS, :], w_out[layer].astype(f32)]
    whole = jnp.concatenate(sides, axis=1)
    below = jnp.zeros((32 - ROWS, WIDE), f32)
    shard[...] = jnp.concatenate([whole, below], axis=0).astype(bf16)


def gate_scale(sqbuf):
    return to_column(lax.rsqrt(sqbuf[3][0:1, :] / DI + epsilon))


def norm_back(gnorm, stream, gain, grad):
    q = row_scale(stream)
    gain_row = jnp.sum(gnorm * stream * q, axis=0, keepdims=True)
    rows = gnorm * gain
    inner = jnp.mean(rows * stream, axis=1, keepdims=True)
    return grad + q * rows - stream * (q * q * q) * inner, gain_row


SCRATCH = {
    "shard0": ((32, WIDE), bf16),
    "shard1": ((32, WIDE), bf16),
    "met0": ((32, WIDE), bf16),
    "met1": ((32, WIDE), bf16),
    "spare": ((128, 128), f32),
    "heads": ((2, 8, 128), f32),
    "weights0": ((D, WIDE), bf16),
    "weights1": ((D, WIDE), bf16),
    "ng0": ((TOK, D), bf16),
    "ng1": ((TOK, D), bf16),
    "gb0": ((TOK, D), bf16),
    "gb1": ((TOK, D), bf16),
    "marks": ((3, TOK, 128), f32),
    "bias": ((TOK, TOK), f32),
    "bias_t": ((TOK, TOK), f32),
    "inner": ((TOK, TOK), f32),
    "dinner": ((TOK, TOK), f32),
    "act": ((TOK, CONV), bf16),
    "xs": ((TOK, UNITS), bf16),
    "d16": ((TOK, UNITS), bf16),
    "mixed": ((TOK, UNITS), bf16),
    "z": ((TOK, UNITS), f32),
    "dsc": ((TOK, UNITS), f32),
    "grads": ((TOK, 1152), bf16),
    "grad_small": ((8, CONV), f32),
    "up": ((TOK, D), bf16),
    "gn": ((TOK, D), bf16),
    "squares": ((8, TOK), f32),
    "tmp": ((2, 2, QUARTER, D), bf16),
    "total": ((OWN, D), f32),
    "stream1": ((OWN, D), f32),
    "branch0": ((OWN, D), f32),
    "grad0": ((OWN, D), f32),
    "gg1": ((8, 128), f32),
    "held": ((4, 32, 128), f32),
    "got": ((13, 32, 128), f32),
}
for layer_name in "01":
    SCRATCH["proj" + layer_name] = ((TOK, 1152), f32)
    SCRATCH["y" + layer_name] = ((TOK, UNITS), f32)
    SCRATCH["logs" + layer_name] = ((TOK, 128), f32)
    SCRATCH["small" + layer_name] = ((8, CONV), f32)
    SCRATCH["sq" + layer_name] = ((4, 8, 128), f32)
    SCRATCH["rk" + layer_name] = ((4, 8, 128), f32)
    SCRATCH["gw" + layer_name] = ((D, WIDE), bf16)
    SCRATCH["head" + layer_name] = ((8, 128), f32)
    SCRATCH["up_got" + layer_name] = ((2, 6, QUARTER, D), bf16)
    SCRATCH["gn_got" + layer_name] = ((2, 6, QUARTER, D), bf16)
SCATTER = [
    ((D, UNITS), bf16),
    ((4, 4, PAIR, UNITS), bf16),
    ((3, 4, PAIR, UNITS), bf16),
    ((4, PAIR, UNITS), bf16),
    ((3, PAIR, UNITS), bf16),
    ((PAIR, UNITS), f32),
    ((ROWS, UNITS), f32),
    ((3, ROWS, UNITS), f32),
]
for layer_name in "01":
    for moment in "el":
        for part, form in enumerate(SCATTER):
            SCRATCH[f"scatter{layer_name}{moment}{part}"] = form
ARGUMENTS = (
    "tokens",
    "gains",
    "cot",
    "step_bias",
    "log_rates",
    "skips",
    "w_zx",
    "w_bc",
    "w_dt",
    "conv_x",
    "conv_bc",
    "gate_gain",
    "w_out",
)
RESULTS = ("block_out", "input_grad", "sum0", "sum1", "values")
COPIES = 336


def whole_kernel(names, *refs):
    a = SimpleNamespace(**dict(zip(names, refs)))
    sources, staged = refs[1:14], [getattr(a, "v_" + name) for name in ARGUMENTS]
    at = Place()
    sems = Sems(a.send, a.recv)
    peers = more_peers(at)
    greet(peers)
    loads = [
        pltpu.make_async_copy(source, target, a.arrived.at[index])
        for index, (source, target) in enumerate(zip(sources, staged))
    ]
    for load in loads:
        load.start()
    for load in loads:
        load.wait()
    tokens, gains, cot, step_bias, log_rates, skips = staged[:6]
    parts = (*staged[6:], a.spare)

    def kept(layer):
        return [getattr(a, name + layer) for name in ("proj", "y", "logs", "small")]

    def forward(layer, ng, weights):
        return forward_steps(
            layer, ng, weights, a.heads, *kept(str(layer)), a.up, a.squares,
            a.marks, a.bias, a.inner, a.act, a.xs,
        )

    def backward(layer, gb, ng, weights, rk, gw, head):
        return backward_steps(
            layer, gb, ng, weights, a.heads, *kept(str(layer)), rk, a.gn, gw, head,
            a.marks, a.bias_t, a.inner, a.dinner, a.act, a.xs, a.d16, a.mixed, a.z, a.dsc,
            a.grads, a.grad_small,
        )

    def scatter(layer, late, gw, out):
        moment = "l" if late else "e"
        sets = [getattr(a, f"scatter{layer}{moment}{part}") for part in range(len(SCATTER))]
        return scatter_weights(at, sems, late, gw, out, *sets)

    pack_shard(0, *parts, a.shard0)
    met_all(peers)
    moving = gather_weights(at, sems, a.shard0, a.met0, a.weights0)
    next(moving)
    stream = tokens[...].astype(f32)
    put_own(at, a.ng0, (stream * row_scale(stream) * gains[0:1, :]).astype(bf16))

    def packing():
        pack_shard(1, *parts, a.shard1)
        a.heads[...] = jnp.zeros(a.heads.shape, f32)
        for layer in range(2):
            for row, values in enumerate((step_bias, log_rates, skips)):
                a.heads[layer, row : row + 1, 0:LOCAL] = values[layer : layer + 1, :]
        fill_masks(a.lengths, a.marks, a.bias, a.bias_t)
        put_own(at, a.gb1, cot[...])
        yield

    together(
        [1, 0, 1, 2, 0, 0, 0, 3, 2, 1, 2],
        moving,
        gather_x(at, sems, a.ng0, 0),
        gather_x(at, sems, a.ng0, 1),
        packing(),
    )

    moving = gather_weights(at, sems, a.shard1, a.met1, a.weights1)
    next(moving)
    sharing = [gather_x(at, sems, a.gb1, part) for part in range(2)]
    together(
        [2, 0, 0, 2, 0, 1, 0, 0, 2, 0, 0, 0, 0],
        forward(0, a.ng0, a.weights0),
        moving,
        sharing[0],
        ends=False,
    )
    column = {}

    def between(part):
        rows = slice(part * HALF, part * HALF + HALF)
        yield from scatter_x(at, sems, a.up, a.up_got0, a.tmp, a.total, part)
        if part == 0:
            column[0] = gate_scale(a.sq0)
        branch = column[0][rows, :] * a.total[rows, :]
        stream = tokens[rows, :].astype(f32) + branch
        a.branch0[rows, :] = branch
        a.stream1[rows, :] = stream
        put_own(at, a.ng1, (stream * row_scale(stream) * gains[1:2, :]).astype(bf16), part)
        yield from gather_x(at, sems, a.ng1, part)

    together(
        [1, 0, 3, 3, 3, 1, 2, 4, 1, 2, 2, 0, 1, 1, 2, 3, 3, 3, 1, 2, 2]
        + [3] * 6
        + [1, 3, 3, 3, 2],
        share_squares(at, sems, a.squares, a.sq0),
        between(0),
        between(1),
        moving,
        sharing[0],
    )

    together(
        [1, 0, 0, 1, 0, 0, 0, 1, 0, 0, 0, 0],
        forward(1, a.ng1, a.weights1),
        sharing[1],
        ends=False,
    )
    back = backward(1, a.gb1, a.ng1, a.weights1, a.rk1, a.gw1, a.head1)
    together(
        [1, 0, 1, 2, 3, 1, 2, 2, 4, 0, 1, 2],
        share_squares(at, sems, a.squares, a.sq1),
        *[scatter_x(at, sems, a.up, a.up_got1, a.tmp, a.total, part) for part in range(2)],
        back,
        sharing[1],
        ends=False,
    )
    r = gate_scale(a.sq1)
    branch = r * a.total[...]
    a.block_out[...] = (a.stream1[...] + branch).astype(bf16)
    dots = jnp.sum(cot[...].astype(f32) * branch, axis=1, keepdims=True)
    put_rows(at, a.rk1, r, r * r * dots / DI)
    together([0, 1, 0], share_rows(at, sems, a.rk1), back, ends=False)
    early, late = (scatter(1, moment, a.gw1, a.sum1) for moment in (False, True))
    together([0, 0, 1, 0, 0, 0, 0, 0, 0, 0], back, early, ends=False)

    def along(part):
        rows = slice(part * HALF, part * HALF + HALF)
        yield from scatter_x(at, sems, a.gn, a.gn_got1, a.tmp, a.total, part)
        grad, gain_row = norm_back(
            a.total[rows, :], a.stream1[rows, :], gains[1:2, :], cot[rows, :].astype(f32)
        )
        low = grad.astype(bf16)
        put_own(at, a.gb0, low, part)
        sharing = gather_x(at, sems, a.gb0, part)
        next(sharing)
        a.grad0[rows, :] = grad
        column[1, part] = jnp.sum(low.astype(f32) * a.branch0[rows, :], axis=1, keepdims=True)
        column[2, part] = gain_row
        sent = iter(())
        if part:
            dots = jnp.concatenate([column[1, 0], column[1, 1]], axis=0)
            put_rows(at, a.rk0, column[0], column[0] * column[0] * dots / DI)
            sent = share_rows(at, sems, a.rk0)
            next(sent)
            gain_row = column[2, 0] + column[2, 1]
            for c in range(6):
                a.gg1[c : c + 1, :] = gain_row[:, c * 128 : c * 128 + 128]
        yield
        yield from sharing
        yield from sent

    last = backward(0, a.gb0, a.ng0, a.weights0, a.rk0, a.gw0, a.head0)
    together(
        [0, 2, 0, 1, 4, 0, 1, 3, 1, 5, 0, 0, 1, 4, 5, 0, 1, 1, 4, 0, 1, 4],
        along(0),
        along(1),
        back,
        last,
        early,
        late,
        ends=False,
    )
    early = scatter(0, False, a.gw0, a.sum0)
    together([0, 0, 0, 1, 0, 0, 2, 0, 0, 1, 0, 2, 0, 0, 2], last, early, late, ends=False)

    def final(part):
        rows = slice(part * HALF, part * HALF + HALF)
        yield from scatter_x(at, sems, a.gn, a.gn_got0, a.tmp, a.total, part)
        grad, gain_row = norm_back(
            a.total[rows, :], tokens[rows, :].astype(f32), gains[0:1, :], a.grad0[rows, :]
        )
        a.input_grad[rows, :] = grad
        column[3, part] = gain_row
        if part == 0:
            return
        gain_row = column[3, 0] + column[3, 1]
        a.values[...] = jnp.zeros(a.values.shape, f32)
        for c in range(6):
            a.values[c : c + 1, :] = gain_row[:, c * 128 : c * 128 + 128]
        a.values[6:12, :] = a.gg1[0:6, :]
        a.values[16:24, :] = a.head0[...]
        a.values[24:32, :] = a.head1[...]
        yield from sum_everywhere(at, sems, a.values, a.held, a.got)

    together(
        [0, 2, 0, 4, 1, 3, 0, 1, 4, 1, 0, 3, 1, 3, 4, 1, 4, 1, 4, 1],
        final(0),
        final(1),
        last,
        early,
        scatter(0, True, a.gw0, a.sum0),
    )


def finish_kernel(
    sum0, sum1, values, block_in, grad_in,
    block_out, input_grad, norm_gain, zx, bc, dt, conv_x, conv_bc, a_log, dt_bias, d_skip, gate_gain, w_out,
):
    block_out[...] = block_in[...]
    input_grad[...] = grad_in[...]
    for layer, total in enumerate((sum0, sum1)):
        for c in range(6):
            norm_gain[layer : layer + 1, c * 128 : c * 128 + 128] = values[
                layer * 6 + c : layer * 6 + c + 1, :
            ]
        row = 16 + 8 * layer
        for k, out in enumerate((a_log, dt_bias, d_skip)):
            out[layer : layer + 1, :] = values[row + k : row + k + 1, 0:LOCAL]
        zx[layer, :, 0, :] = total[:, 0:UNITS]
        zx[layer, :, 1, :] = total[:, UNITS:768]
        bc[layer] = total[:, 768:1024]
        w_out[layer] = total[:, 1152:]
        spread = total[:, 1024:1152]
        wide = jnp.concatenate([spread, jnp.zeros((128 - ROWS, 128), f32)], axis=0).T
        dt[:, layer, :] = wide[0:LOCAL, 0:ROWS]
        small = total[0:1, 1024:1152]
        at = LOCAL
        for tap in range(5):
            for e in range(2):
                conv_x[layer, tap, e : e + 1, :] = small[:, at : at + LOCAL]
                at += LOCAL
        for tap in range(5):
            conv_bc[tap, layer : layer + 1, :] = small[:, at : at + 8]
            at += 8
        for e in range(2):
            gate_gain[layer, e : e + 1, :] = small[:, at : at + LOCAL]
            at += LOCAL


def body(
    tokens,
    lengths,
    norm_gain,
    w_zx,
    w_bc,
    w_dt,
    conv_x,
    conv_bc,
    a_log,
    dt_bias,
    d_skip,
    gate_gain,
    w_out,
    cotangent,
):
    arguments = (
        tokens,
        norm_gain,
        cotangent,
        dt_bias,
        a_log,
        d_skip,
        w_zx,
        w_bc,
        w_dt.transpose(2, 0, 1),
        conv_x.swapaxes(2, 3),
        conv_bc.swapaxes(0, 1),
        gate_gain.swapaxes(1, 2),
        w_out.swapaxes(1, 2),
    )
    results = [
        shaped((OWN, D), bf16),
        shaped((OWN, D)),
        shaped((ROWS, WIDE)),
        shaped((ROWS, WIDE)),
        shaped((32, 128)),
    ]
    names = ["lengths", *ARGUMENTS, *RESULTS, *("v_" + name for name in ARGUMENTS), *SCRATCH]
    names += ["arrived", "send", "recv"]
    block_out, input_grad, sum0, sum1, values = pl.pallas_call(
        functools.partial(whole_kernel, names),
        out_shape=results,
        in_specs=[pl.BlockSpec(memory_space=pltpu.SMEM)]
        + [pl.BlockSpec(memory_space=pltpu.HBM)] * len(arguments),
        out_specs=[VM] * len(results),
        scratch_shapes=[pltpu.VMEM(argument.shape, argument.dtype) for argument in arguments]
        + [pltpu.VMEM(shape, kind) for shape, kind in SCRATCH.values()]
        + [
            pltpu.SemaphoreType.DMA((len(arguments),)),
            pltpu.SemaphoreType.DMA((COPIES,)),
            pltpu.SemaphoreType.DMA((COPIES,)),
        ],
        compiler_params=pltpu.CompilerParams(
            collective_id=0, has_side_effects=True, vmem_limit_bytes=LIMIT
        ),
    )(lengths, *arguments)
    outs = pl.pallas_call(
        finish_kernel,
        out_shape=[
            shaped((OWN, D), bf16),
            shaped((OWN, D)),
            shaped((2, D)),
            shaped((2, ROWS, 2, UNITS)),
            shaped((2, ROWS, 256)),
            shaped((LOCAL, 2, ROWS)),
            shaped((2, 5, 2, LOCAL)),
            shaped((5, 2, 8)),
            shaped((2, LOCAL)),
            shaped((2, LOCAL)),
            shaped((2, LOCAL)),
            shaped((2, 2, LOCAL)),
            shaped((2, ROWS, UNITS)),
        ],
        in_specs=[VM] * 5,
        out_specs=[VM] * 13,
        compiler_params=pltpu.CompilerParams(vmem_limit_bytes=LIMIT),
    )(sum0, sum1, values, block_out, input_grad)
    block_out, input_grad, g_norm, g_zx, g_bc, g_dt, g_cx, g_cb, g_a, g_b, g_d, g_gate, g_out = outs
    return (
        block_out,
        input_grad,
        g_norm,
        g_zx,
        g_bc,
        g_dt.transpose(1, 2, 0),
        g_cx.swapaxes(2, 3),
        g_cb.swapaxes(0, 1),
        g_a,
        g_b,
        g_d,
        g_gate.swapaxes(1, 2),
        g_out.swapaxes(1, 2),
    )


def solution(mesh):
    return jax.shard_map(
        body,
        mesh=mesh,
        in_specs=(
            P(("dp", "tensor"), None),
            P("dp", None),
            P(),
            P(None, "dp", None, "tensor"),
            P(None, "dp", None),
            P(None, "dp", "tensor"),
            P(None, None, "tensor", "dp"),
            P(None, None, "dp"),
            P(None, "tensor"),
            P(None, "tensor"),
            P(None, "tensor"),
            P(None, "tensor", "dp"),
            P(None, "tensor", "dp"),
            P(("dp", "tensor"), None),
        ),
        out_specs=(
            P(("dp", "tensor"), None),
            P(("dp", "tensor"), None),
            P(),
            P(None, "dp", None, "tensor"),
            P(None, "dp", None),
            P(None, "dp", "tensor"),
            P(None, None, "tensor", "dp"),
            P(None, None, "dp"),
            P(None, "tensor"),
            P(None, "tensor"),
            P(None, "tensor"),
            P(None, "tensor", "dp"),
            P(None, "tensor", "dp"),
        ),
        check_vma=False,
    )
```
